512 devices in a mesh: img: 16 (over x, z_hi, core), txt: 32 (over y, z_lo).
Axes of the slice: x: 4, y: 4, z: 16 (z_hi: 2, z_lo: 8; z = z_hi * 8 + z_lo), core: 2. Of those that a mesh axis runs over, the one named last changes fastest.
Arguments:
- images: bfloat16 [9216, 1152], P(('img', 'txt')), may hold values from -8 to 8
- texts: bfloat16 [9216, 1152], P('txt', 'img'), may hold values from -8 to 8
- logit_scale: float32 [1], replicated, may hold values from 48 to 115
- bias: float32 [1], replicated, may hold values from -40 to 0
Outputs:
- loss: float32 [1], replicated
- grad_images: float32 [9216, 1152], P(('img', 'txt'))
- grad_texts: float32 [9216, 1152], P('txt', 'img')
The draws below stay inside these ranges and needn't reach their ends.
All inputs are finite; a program needn't handle non-finite values.
Results may differ from the reference program's by a relative error of at most 0.033.
Values may be sent and summed in bfloat16 or wider, within the bound.
A program may use at most 64 MiB of HBM per device.

```python
import math
import jax
import jax.numpy as jnp
from jax import lax

D = 1152
PAIRS = 9216
IMG_BLOCK = 576
TXT_BLOCK = 288
N_IMG = 16
N_TXT = 32


def shared_rows(key):
    inner_key = jax.random.fold_in(key, 101)
    first, second = jax.random.split(inner_key)
    jitter = jax.random.uniform(first, (PAIRS, 1), jnp.float32, 0.7, 1.0)
    position = jnp.arange(PAIRS, dtype=jnp.float32)[:, None] / float(PAIRS)
    strength = 1.5 * (1.0 - position) * jitter
    common = jax.random.normal(second, (PAIRS, D), jnp.float32)
    return strength * common


def sharp_pair(key):
    inner_key = jax.random.fold_in(key, 202)
    first, second = jax.random.split(inner_key)
    mixing = jax.random.uniform(first, (1,), jnp.float32)
    shifted = jax.random.uniform(second, (1,), jnp.float32, -0.5, 1.5)
    lowest = float(D // 24)
    highest = float(D // 10)
    sharp = lowest + (highest - lowest) * mixing
    offset = -jnp.log(jnp.float32(PAIRS)) - sharp * sharp / (2.0 * D) + shifted
    return (sharp, offset)


def noisy_rows(key, lowest, highest):
    first, second = jax.random.split(key)
    noise = jax.random.normal(first, (PAIRS, D), jnp.float32)
    level = jnp.exp(jax.random.uniform(second, (PAIRS, 1), jnp.float32, math.log(lowest), math.log(highest)))
    return (noise, level)


def draw_images(key, part):
    shared = shared_rows(key)
    key = jax.random.fold_in(key, 11)
    first = jax.random.fold_in(key, 0)
    noise, level = noisy_rows(first, 0.4, 4.0)
    raw = (shared + noise) * level
    return jnp.clip(raw, -8.0, 8.0).astype(jnp.bfloat16)


def draw_texts(key, part):
    shared = shared_rows(key)
    key = jax.random.fold_in(key, 12)
    noise, level = noisy_rows(key, 0.4, 4.0)
    raw = (shared + noise) * level
    return jnp.clip(raw, -8.0, 8.0).astype(jnp.bfloat16)


def draw_logit_scale(key, part):
    sharp, offset = sharp_pair(key)
    return sharp.astype(jnp.float32)


def draw_bias(key, part):
    sharp, offset = sharp_pair(key)
    return offset.astype(jnp.float32)


def setup_inputs(seed: int = 0) -> dict:
    keys = jax.random.split(jax.random.key(seed), 5)
    return {
        "images": draw_images(jax.random.fold_in(keys[4], 71), 0),
        "texts": draw_texts(jax.random.fold_in(keys[4], 71), 0),
        "logit_scale": draw_logit_scale(jax.random.fold_in(keys[4], 71), 0),
        "bias": draw_bias(jax.random.fold_in(keys[4], 71), 0),
    }


EPS = 1e-06

def unit_rows(raw):
    wide = raw.astype(jnp.float32)
    norms = lax.rsqrt(lax.optimization_barrier(jnp.sum(wide * wide, axis=1)) + EPS)
    return ((wide * norms[:, None]).astype(jnp.bfloat16), norms)

def back_rows(raw, norms, upstream):
    wide = raw.astype(jnp.float32)
    inner = lax.optimization_barrier(jnp.sum(wide * upstream, axis=1))
    return norms[:, None] * upstream - wide * (norms * norms * norms * inner)[:, None]

def reference(images, texts, logit_scale, bias):
    sharpness = logit_scale[0]
    offset = bias[0]
    x_unit, x_norm = unit_rows(images)
    y_unit, y_norm = unit_rows(texts)
    y_blocks = y_unit.reshape(N_TXT, TXT_BLOCK, D)

    def image_block(carry, block_img):
        txt_acc, loss_acc = carry
        x_block = lax.dynamic_slice_in_dim(x_unit, block_img * IMG_BLOCK, IMG_BLOCK, 0)

        def text_block(img_acc, block_txt):
            y_block = y_blocks[block_txt]
            logits = sharpness * lax.dot_general(x_block, y_block, (((1,), (1,)), ((), ())), preferred_element_type=jnp.float32) + offset
            rows_here = block_img * IMG_BLOCK + jnp.arange(IMG_BLOCK, dtype=jnp.int32)
            cols_here = block_txt * TXT_BLOCK + jnp.arange(TXT_BLOCK, dtype=jnp.int32)
            labels = jnp.where(rows_here[:, None] == cols_here[None, :], jnp.float32(1.0), jnp.float32(-1.0))
            loss_part = jnp.sum(jax.nn.softplus(-labels * logits))
            weights = (-labels * jax.nn.sigmoid(-labels * logits) * sharpness).astype(jnp.bfloat16)
            img_part = jnp.dot(weights, y_block, preferred_element_type=jnp.float32).astype(jnp.bfloat16)
            img_part = lax.optimization_barrier(img_part).astype(jnp.float32)
            txt_part = lax.dot_general(weights, x_block, (((0,), (0,)), ((), ())), preferred_element_type=jnp.float32).astype(jnp.bfloat16)
            txt_part = lax.optimization_barrier(txt_part).astype(jnp.float32)
            return (img_acc + img_part, (txt_part, loss_part))
        img_sum, (txt_parts, losses) = lax.scan(text_block, jnp.zeros((IMG_BLOCK, D), jnp.float32), jnp.arange(N_TXT, dtype=jnp.int32))
        return ((txt_acc + txt_parts, loss_acc + jnp.sum(losses)), img_sum)
    start = (jnp.zeros((N_TXT, TXT_BLOCK, D), jnp.float32), jnp.zeros((), jnp.float32))
    (txt_acc, loss_sum), img_sums = lax.scan(image_block, start, jnp.arange(N_IMG, dtype=jnp.int32))
    d_img = img_sums.reshape(PAIRS, D)
    d_txt = txt_acc.reshape(PAIRS, D)
    grad_images = back_rows(images, x_norm, d_img)
    grad_texts = back_rows(texts, y_norm, d_txt)
    loss = (loss_sum / PAIRS).reshape(1)
    return (loss, grad_images, grad_texts)
```

```python
import functools

import jax
import jax.numpy as jnp
from jax import lax
from jax.experimental import pallas as pl
from jax.experimental.pallas import tpu as pltpu
from jax.sharding import PartitionSpec as P

EPS = 1e-06
F32 = jnp.float32
BF16 = jnp.bfloat16
MESH = pl.DeviceIdType.MESH
D = 1152
PAIRS = 9216
ROWS = 18
SLAB = 72
SLABP = 80
COLS = 72
TXT = 288
PIECE = 80


def dot(a, b, dims):
    return lax.dot_general(a, b, (dims, ((), ())), preferred_element_type=F32)


def pack(data, inner):
    high = inner.astype(BF16).astype(F32)
    low = inner - high
    row = lax.broadcasted_iota(jnp.int32, (8, TXT), 0)
    tail = jnp.where(row == 0, high, jnp.where(row == 1, low, 0.0))
    return jnp.concatenate([data, tail], axis=0).astype(BF16)


def unpack(piece):
    wide = piece.astype(F32)
    return wide[:COLS], wide[COLS : COLS + 1] + wide[COLS + 1 : COLS + 2]


def kernel(
    images, texts, scale, bias, loss_out, img_out, txt_out,
    xz, xf, xs, ts, tt, inv_txt, w1, iy_send, iy_recv, iown, iz_send, iz_recv,
    dtf, cs_send, cs_recv, tx_send, tx_recv, tx_own, tb_send, tb_recv, tb_own, th_send, th_recv,
    pad_a, pad_b, ls,
    xz_ss, xz_rs, xs_ss, xs_rs, ts_ss, ts_rs, iy_ss, iy_rs, iz_ss, iz_rs,
    cs_ss, cs_rs, tx_ss, tx_rs, tb_ss, tb_rs, th_ss, th_rs, ls_ss, ls_rs,
):
    i = lax.axis_index("img")
    t = lax.axis_index("txt")
    x, zh, c = i // 4, (i // 2) % 2, i % 2
    y, zm, zb = t // 8, (t // 2) % 4, t % 2
    zbp, zhp, cp = 1 - zb, 1 - zh, 1 - c

    def dev(x=x, zh=zh, c=c, y=y, zm=zm, zb=zb):
        return (x * 4 + zh * 2 + c, y * 8 + zm * 2 + zb)

    def turn(v, d):
        return lax.rem(v + d, 4)

    order = (1, 3, 2)
    peers = [dev(zh=zhp), dev(zb=zbp), dev(c=cp)]
    for d in order:
        peers += [dev(x=turn(x, d)), dev(y=turn(y, d)), dev(zm=turn(zm, d))]
    barrier = pltpu.get_barrier_semaphore()
    for peer in peers:
        pl.semaphore_signal(barrier, inc=1, device_id=peer, device_id_type=MESH)

    pending = []

    def copy(src, dst, ss, rs, peer):
        return pltpu.make_async_remote_copy(
            src_ref=src, dst_ref=dst, send_sem=ss, recv_sem=rs, device_id=peer, device_id_type=MESH
        )

    def send(*args):
        one = copy(*args)
        one.start()
        pending.append(one)

    sharpness = scale[0]
    offset = bias[0]

    pad_a[0:TXT, 0:COLS] = texts[...].astype(F32)
    ts[zb, x, zh, c] = pad_a[...].T[0:COLS, 0:TXT].astype(BF16)
    own_image = images[...].astype(F32)
    img_norm = lax.rsqrt(jnp.sum(own_image * own_image, axis=1, keepdims=True) + EPS)
    xz[zm] = (own_image * img_norm).astype(BF16)

    pl.semaphore_wait(barrier, len(peers))

    slots = [0]

    def t_send(b, xx, h, peer):
        k = slots[0]
        slots[0] += 1
        send(ts.at[b, xx, h, c], ts.at[b, xx, h, c], ts_ss.at[k], ts_rs.at[b, xx, h, c], peer)

    def t_wait(b, xx, h, cc):
        ref = ts.at[b, xx, h, cc]
        copy(ref, ref, ts_ss.at[0], ts_rs.at[b, xx, h, cc], dev(c=cp)).wait_recv()

    def to_x(b, h):
        for d in order:
            t_send(b, x, h, dev(x=turn(x, d)))

    def to_c(b, xx, h):
        t_send(b, xx, h, dev(c=cp))

    t_send(zb, x, zh, dev(zh=zhp))
    t_send(zb, x, zh, dev(zb=zbp))
    for k, d in enumerate((2, 1, 3)):
        send(xz.at[zm], xz.at[zm], xz_ss.at[k], xz_rs.at[zm], dev(zm=turn(zm, d)))
    to_x(zb, zh)
    to_c(zb, x, zh)
    t_wait(zbp, x, zh, c)
    to_x(zbp, zh)
    to_c(zbp, x, zh)

    for d in order:
        q = turn(zm, d)
        copy(xz.at[q], xz.at[q], xz_ss.at[0], xz_rs.at[q], dev(zm=q)).wait_recv()
    for q in range(4):
        xf[q * ROWS : (q + 1) * ROWS, :] = xz[q].astype(F32)
    xf[SLAB:SLABP, :] = jnp.zeros((SLABP - SLAB, D), F32)
    xs[y] = xf[...].astype(BF16)
    for k, d in enumerate((2, 1, 3)):
        send(xs.at[y], xs.at[y], xs_ss.at[k], xs_rs.at[y], dev(y=turn(y, d)))

    t_wait(zb, x, zhp, c)
    t_send(zb, x, zhp, dev(zb=zbp))
    to_x(zb, zhp)
    to_c(zb, x, zhp)
    t_wait(zbp, x, zhp, c)
    to_x(zbp, zhp)
    to_c(zbp, x, zhp)
    for b, h in ((zb, zh), (zbp, zh), (zb, zhp), (zbp, zhp)):
        for d in order:
            xx = turn(x, d)
            t_wait(b, xx, h, c)
            to_c(b, xx, h)
    for b, h in ((zb, zh), (zbp, zh), (zb, zhp), (zbp, zhp)):
        for d in (0, 1, 3, 2):
            t_wait(b, turn(x, d), h, cp)
    for b in range(2):
        square = jnp.zeros((8, TXT), F32)
        for j in range(8):
            both = jnp.concatenate(
                [ts[b, j // 2, j % 2, 0].astype(F32), ts[b, j // 2, j % 2, 1].astype(F32)], axis=0
            )
            tt[b, j * 144 : (j + 1) * 144, :] = both.astype(BF16)
            square += jnp.sum((both * both).reshape(18, 8, TXT), axis=0)
        inv_txt[b] = lax.rsqrt(jnp.sum(square, axis=0, keepdims=True) + EPS)

    row = lax.broadcasted_iota(jnp.int32, (SLABP, TXT), 0)
    col = lax.broadcasted_iota(jnp.int32, (SLABP, TXT), 1)
    gap = (row >= 18).astype(jnp.int32) + (row >= 36).astype(jnp.int32) + (row >= 54).astype(jnp.int32)
    row_in = row + 18 * gap - col + (i * 576 + zb * 18 - (y * 8 + zm * 2) * TXT)
    valid = row < SLAB
    loss_row = jnp.zeros((1, TXT), F32)
    inner = [jnp.zeros((1, TXT), F32) for _ in range(2)]
    for k, d in enumerate((0, 1, 3, 2)):
        yy = turn(y, d)
        if d:
            copy(xs.at[yy], xs.at[yy], xs_ss.at[0], xs_rs.at[yy], dev(y=yy)).wait_recv()
        slab = xs[yy]
        term = jnp.zeros((SLABP, D), F32)
        for b in range(2):
            raw = dot(slab, tt[b], ((1,), (0,)))
            logits = raw * (sharpness * inv_txt[b]) + offset
            diagonal = row_in == b * TXT - yy * 144
            sign = jnp.where(diagonal, -1.0, 1.0)
            u = sign * logits
            e = jnp.exp(-jnp.abs(u))
            soft = jnp.maximum(u, 0.0) + jnp.log1p(e)
            loss_row += jnp.sum(jnp.where(valid, soft, 0.0), axis=0, keepdims=True)
            w = sign * (jnp.where(u >= 0, 1.0, e) / (1.0 + e)) * sharpness
            w = jnp.where(valid, w, 0.0)
            wb = w.astype(BF16)
            inner[b] += jnp.sum(wb.astype(F32) * raw, axis=0, keepdims=True)
            w1[b, yy] = wb
            term += dot((w * inv_txt[b]).astype(BF16), tt[b], ((1,), (1,)))
        if d:
            iy_send[yy] = term.astype(BF16)
            send(iy_send.at[yy], iy_recv.at[y], iy_ss.at[k], iy_rs.at[y], dev(y=yy))
        else:
            iown[...] = term

    def loss_send(stage, place, others, value):
        ls[stage, place] = jnp.full((8, 128), value, F32)
        for k, peer in enumerate(others):
            send(ls.at[stage, place], ls.at[stage, place], ls_ss.at[stage, k], ls_rs.at[stage, place], peer)

    def loss_wait(stage, places, n):
        for q in places:
            copy(ls.at[stage, q], ls.at[stage, q], ls_ss.at[stage, 0], ls_rs.at[stage, q], dev(c=cp)).wait_recv()
        total = ls[stage, 0]
        for q in range(1, n):
            total += ls[stage, q]
        return total

    loss_send(0, c, [dev(c=cp)], jnp.sum(loss_row))

    for b in range(2):
        weights = w1[b].reshape(4 * SLABP, TXT)
        for q in range(3):
            part = xs[:, :, q * 384 : (q + 1) * 384].reshape(4 * SLABP, 384)
            dtf[b, q * 384 : (q + 1) * 384, :] = dot(part, weights, ((0,), (0,)))

    def features(b, xx, h, cc):
        return dtf[b, pl.ds(pl.multiple_of((xx * 4 + h * 2 + cc) * COLS, 8), COLS), :]

    for b in range(2):
        for xx in range(4):
            for h in range(2):
                cs_send[b, xx, h] = pack(features(b, xx, h, cp), inner[b])
                send(cs_send.at[b, xx, h], cs_recv.at[b, xx, h], cs_ss.at[b, xx, h], cs_rs.at[b, xx, h], dev(c=cp))

    loss_v = loss_wait(0, [cp], 2)
    loss_send(1, y, [dev(y=turn(y, d)) for d in order], loss_v)

    total = iown[...]
    for d in order:
        q = turn(y, d)
        copy(iy_recv.at[q], iy_recv.at[q], iy_ss.at[0], iy_rs.at[q], dev(y=q)).wait_recv()
        total += iy_recv[q].astype(F32)
    xf[...] = total
    for q in range(4):
        iz_send[q] = xf[q * ROWS : (q + 1) * ROWS, :].astype(BF16)
    for k, d in enumerate((2, 1, 3)):
        q = turn(zm, d)
        send(iz_send.at[q], iz_recv.at[zm], iz_ss.at[k], iz_rs.at[zm], dev(zm=q))
    loss_v = loss_wait(1, [turn(y, d) for d in order], 4)
    loss_send(2, zm, [dev(zm=turn(zm, d)) for d in order], loss_v)

    for d in (1, 3, 2, 0):
        xx = turn(x, d)
        for k, (b, h) in enumerate(((zbp, zhp), (zb, zhp), (zbp, zh), (zb, zh))):
            ref = cs_recv.at[b, xx, h]
            copy(ref, ref, cs_ss.at[0, 0, 0], cs_rs.at[b, xx, h], dev(c=cp)).wait_recv()
            data, inn = unpack(cs_recv[b, xx, h])
            own_inn = jnp.where(b == 0, inner[0], inner[1])
            data += features(b, xx, h, c)
            inn += own_inn
            if d:
                tx_send[xx, b, h] = pack(data, inn)
                send(tx_send.at[xx, b, h], tx_recv.at[x, b, h], tx_ss.at[d, k], tx_rs.at[x, b, h], dev(x=xx))
            else:
                tx_own[b, h, 0:COLS] = data
                tx_own[b, h, COLS:PIECE] = jnp.broadcast_to(inn, (8, TXT))

    q0 = iz_send[zm].astype(F32)
    for d in order:
        q = turn(zm, d)
        copy(iz_recv.at[q], iz_recv.at[q], iz_ss.at[0], iz_rs.at[q], dev(zm=q)).wait_recv()
        q0 += iz_recv[q].astype(F32)
    own_image = images[...].astype(F32)
    img_norm = lax.rsqrt(jnp.sum(own_image * own_image, axis=1, keepdims=True) + EPS)
    img_inner = jnp.sum(own_image * q0, axis=1, keepdims=True)
    img_out[...] = img_norm * q0 - own_image * (img_norm * img_norm * img_norm * img_inner)
    loss_v = loss_wait(2, [turn(zm, d) for d in order], 4)
    loss_send(3, x, [dev(x=turn(x, d)) for d in order], loss_v)

    def over_x(b, h):
        data = tx_own[b, h, 0:COLS]
        inn = tx_own[b, h, COLS : COLS + 1]
        for d in order:
            xx = turn(x, d)
            ref = tx_recv.at[xx, b, h]
            copy(ref, ref, tx_ss.at[1, 0], tx_rs.at[xx, b, h], dev(x=xx)).wait_recv()
            more, more_inn = unpack(tx_recv[xx, b, h])
            data += more
            inn += more_inn
        return data, inn

    for k, h in enumerate((zhp, zh)):
        tb_send[h] = pack(*over_x(zbp, h))
        send(tb_send.at[h], tb_recv.at[h], tb_ss.at[k], tb_rs.at[h], dev(zb=zbp))
    loss_v = loss_wait(3, [turn(x, d) for d in order], 4)
    loss_send(4, zb, [dev(zb=zbp)], loss_v)

    def over_pair(h):
        data, inn = over_x(zb, h)
        copy(tb_recv.at[h], tb_recv.at[h], tb_ss.at[0], tb_rs.at[h], dev(zb=zbp)).wait_recv()
        more, more_inn = unpack(tb_recv[h])
        return data + more, inn + more_inn

    th_send[...] = pack(*over_pair(zhp))
    send(th_send, th_recv, th_ss, th_rs, dev(zh=zhp))
    loss_v = loss_wait(4, [zbp], 2)
    loss_send(5, zh, [dev(zh=zhp)], loss_v)
    data, inn = over_pair(zh)
    copy(th_recv, th_recv, th_ss, th_rs, dev(zh=zhp)).wait_recv()
    more, more_inn = unpack(th_recv[...])
    data += more
    inn += more_inn
    norm = inv_txt[zb]
    grad = norm * data - ts[zb, x, zh, c].astype(F32) * (norm * norm * norm * inn)
    pad_b[0:COLS, 0:TXT] = grad
    txt_out[...] = pad_b[...].T[0:TXT, 0:COLS]
    loss_v = loss_wait(5, [zhp], 2)
    loss_out[0] = jnp.max(loss_v) / PAIRS
    for one in pending:
        one.wait_send()


def per_device(images, texts, logit_scale, bias):
    vmem = pl.BlockSpec(memory_space=pltpu.VMEM)
    smem = pl.BlockSpec(memory_space=pltpu.SMEM)
    sem = pltpu.SemaphoreType.DMA
    return pl.pallas_call(
        kernel,
        out_shape=(
            jax.ShapeDtypeStruct((1,), F32),
            jax.ShapeDtypeStruct((ROWS, D), F32),
            jax.ShapeDtypeStruct((TXT, COLS), F32),
        ),
        in_specs=[vmem, vmem, smem, smem],
        out_specs=(smem, vmem, vmem),
        scratch_shapes=[
            pltpu.VMEM((4, ROWS, D), BF16),
            pltpu.VMEM((SLABP, D), F32),
            pltpu.VMEM((4, SLABP, D), BF16),
            pltpu.VMEM((2, 4, 2, 2, COLS, TXT), BF16),
            pltpu.VMEM((2, D, TXT), BF16),
            pltpu.VMEM((2, 1, TXT), F32),
            pltpu.VMEM((2, 4, SLABP, TXT), BF16),
            pltpu.VMEM((4, SLABP, D), BF16),
            pltpu.VMEM((4, SLABP, D), BF16),
            pltpu.VMEM((SLABP, D), F32),
            pltpu.VMEM((4, ROWS, D), BF16),
            pltpu.VMEM((4, ROWS, D), BF16),
            pltpu.VMEM((2, D, TXT), F32),
            pltpu.VMEM((2, 4, 2, PIECE, TXT), BF16),
            pltpu.VMEM((2, 4, 2, PIECE, TXT), BF16),
            pltpu.VMEM((4, 2, 2, PIECE, TXT), BF16),
            pltpu.VMEM((4, 2, 2, PIECE, TXT), BF16),
            pltpu.VMEM((2, 2, PIECE, TXT), F32),
            pltpu.VMEM((2, PIECE, TXT), BF16),
            pltpu.VMEM((2, PIECE, TXT), BF16),
            pltpu.VMEM((2, PIECE, TXT), F32),
            pltpu.VMEM((PIECE, TXT), BF16),
            pltpu.VMEM((PIECE, TXT), BF16),
            pltpu.VMEM((384, 128), F32),
            pltpu.VMEM((128, 384), F32),
            pltpu.VMEM((6, 4, 8, 128), F32),
            sem((3,)), sem((4,)),
            sem((3,)), sem((4,)),
            sem((32,)), sem((2, 4, 2, 2)),
            sem((4,)), sem((4,)),
            sem((3,)), sem((4,)),
            sem((2, 4, 2)), sem((2, 4, 2)),
            sem((4, 4)), sem((4, 2, 2)),
            sem((2,)), sem((2,)),
            sem, sem,
            sem((6, 3)), sem((6, 4)),
        ],
        compiler_params=pltpu.CompilerParams(
            collective_id=0, has_side_effects=True, vmem_limit_bytes=48 * 1024 * 1024
        ),
        name="siglip",
    )(images, texts, logit_scale, bias)


def solution(mesh):
    return jax.shard_map(
        per_device,
        mesh=mesh,
        in_specs=(P(("img", "txt"), None), P("txt", "img"), P(), P()),
        out_specs=(P(), P(("img", "txt"), None), P("txt", "img")),
        check_vma=False,
    )
```

```python
import jax
import jax.numpy as jnp
from jax import lax
from jax.experimental import pallas as pl
from jax.experimental.pallas import tpu as pltpu
from jax.sharding import PartitionSpec as P

EPS = 1e-06
F32 = jnp.float32
BF16 = jnp.bfloat16
MESH = pl.DeviceIdType.MESH
D = 1152
PAIRS = 9216
ROWS = 18
HALF = 72
SLAB = 144
COLS = 72
TXT = 288
PIECE = 80


def dot(a, b, dims):
    return lax.dot_general(a, b, (dims, ((), ())), preferred_element_type=F32)


def pack(data, inner):
    high = inner.astype(BF16).astype(F32)
    low = inner - high
    row = lax.broadcasted_iota(jnp.int32, (8, TXT), 0)
    tail = jnp.where(row == 0, high, jnp.where(row == 1, low, 0.0))
    return jnp.concatenate([data, tail], axis=0).astype(BF16)


def unpack(piece):
    wide = piece.astype(F32)
    return wide[:COLS], wide[COLS : COLS + 1] + wide[COLS + 1 : COLS + 2]


def kernel(
    images, texts, scale, bias, loss_out, img_out, txt_out,
    xz, xf, xs, ts, tt, inv_own, inv_far, w1, term, iown, ic_send, ic_recv, iy_send, iy_recv, iz_send, iz_recv,
    dtf, tx_send, tx_recv, tacc, tb_send, tb_recv, tf_send, tf_recv, fin, ls,
    xz_ss, xz_rs, xc_ss, xc_rs, ts_ss, ts_rs, inv_ss, inv_rs, ic_ss, ic_rs, iy_ss, iy_rs, iz_ss, iz_rs,
    tx_ss, tx_rs, tb_ss, tb_rs, tf_ss, tf_rs, ls_ss, ls_rs,
):
    i = lax.axis_index("img")
    t = lax.axis_index("txt")
    x, zh, c = i // 4, (i // 2) % 2, i % 2
    y, zm, zb = t // 8, (t // 2) % 4, t % 2
    zbp, zhp, cp = 1 - zb, 1 - zh, 1 - c
    is_home = c == zb
    is_guest = c != zb

    def dev(x=x, zh=zh, c=c, y=y, zm=zm, zb=zb):
        return (x * 4 + zh * 2 + c, y * 8 + zm * 2 + zb)

    def turn(v, d):
        return lax.rem(v + d, 4)

    near = zm + 1 - 2 * (zm % 2)
    far = turn(zm, 2)
    last = turn(near, 2)
    order = (1, 3, 2)
    peers = [dev(c=cp)]
    for cc in range(2):
        peers += [dev(zh=zhp, c=cc), dev(zb=zbp, c=cc)]
    for d in order:
        peers += [dev(x=turn(x, d)), dev(y=turn(y, d)), dev(zm=turn(zm, d))]
    barrier = pltpu.get_barrier_semaphore()
    for peer in peers:
        pl.semaphore_signal(barrier, inc=1, device_id=peer, device_id_type=MESH)

    pending = {"all": [], "home": [], "guest": []}

    def copy(src, dst, ss, rs, peer):
        return pltpu.make_async_remote_copy(
            src_ref=src, dst_ref=dst, send_sem=ss, recv_sem=rs, device_id=peer, device_id_type=MESH
        )

    def send(src, dst, ss, rs, peer, who="all", like=None):
        copy(src, dst, ss[0].at[ss[1:]] if ss[1:] else ss[0], rs, peer).start()
        pending[who].append((like or (lambda: src), ss))

    def sent(who):
        for like, ss in pending[who]:
            ref = like()
            copy(ref, ref, ss[0].at[ss[1:]] if ss[1:] else ss[0], ls_rs.at[0, 0], dev(c=cp)).wait_send()

    def arrived(ref, rs):
        copy(ref, ref, ls_ss.at[0, 0], rs, dev(c=cp)).wait_recv()

    sharpness = scale[0]
    offset = bias[0]

    own_image = images[...].astype(F32)
    img_norm = lax.rsqrt(jnp.sum(own_image * own_image, axis=1, keepdims=True) + EPS)
    xz[y, c, zm] = (own_image * img_norm).astype(BF16)

    pl.semaphore_wait(barrier, len(peers))

    counts = {"home": 0, "guest": 0}

    def t_send(who, xx, h, cc, peer, own=False):
        k = counts[who]
        counts[who] += 1
        slot = ts.at[xx, h, cc]
        send(texts if own else slot, slot, (ts_ss, k), ts_rs.at[xx, h, cc], peer, who, lambda: texts)

    def t_wait(xx, h, cc):
        arrived(ts.at[xx, h, cc], ts_rs.at[xx, h, cc])

    def t_over_x(who, h, cc, own=False):
        for d in (2, 1, 3):
            t_send(who, x, h, cc, dev(x=turn(x, d)), own)

    x_count = [0]

    def x_send(q, peer):
        k = x_count[0]
        x_count[0] += 1
        slot = xz.at[y, c, q]
        send(slot, slot, (xz_ss, k), xz_rs.at[y, q], peer)

    def x_wait(yy, q):
        arrived(xz.at[yy, c, q], xz_rs.at[yy, q])

    def x_over_y(q):
        for d in (2, 1, 3):
            x_send(q, dev(y=turn(y, d)))

    def x_to_core(k, yy):
        group = xz.at[yy, c]
        send(group, group, (xc_ss, k), xc_rs.at[yy], dev(c=cp))

    @pl.when(is_home)
    def _():
        t_send("home", x, zh, c, dev(zh=zhp), True)
        t_send("home", x, zh, c, dev(zb=zbp), True)
        t_over_x("home", zh, c, True)
        ts[x, zh, c] = texts[...]

    @pl.when(is_guest)
    def _():
        t_send("guest", x, zh, c, dev(zh=zhp, c=cp), True)
        t_send("guest", x, zh, c, dev(zb=zbp, c=cp), True)
        t_send("guest", x, zh, c, dev(c=cp), True)

    x_send(zm, dev(zm=far))
    x_send(zm, dev(zm=near))
    x_over_y(zm)

    @pl.when(is_home)
    def _():
        t_wait(x, zh, cp)
        t_over_x("home", zh, cp)

    @pl.when(is_guest)
    def _():
        for cc in range(2):
            t_wait(x, zh, cc)
            t_over_x("guest", zh, cc)

    x_wait(y, near)
    x_over_y(near)
    x_wait(y, far)
    x_send(far, dev(zm=near))
    x_over_y(far)

    @pl.when(is_home)
    def _():
        for cc in range(2):
            t_wait(x, zhp, cc)
            t_send("home", x, zhp, cc, dev(zb=zbp))
            t_over_x("home", zhp, cc)

    x_wait(y, last)
    x_over_y(last)
    x_to_core(0, y)

    @pl.when(is_guest)
    def _():
        for cc in range(2):
            t_wait(x, zhp, cc)
            t_over_x("guest", zhp, cc)

    for d in order:
        yy = turn(y, d)
        for q in range(4):
            x_wait(yy, turn(zm, q))
        x_to_core(d, yy)
    for h in (zh, zhp):
        for cc in range(2):
            for d in order:
                t_wait(turn(x, d), h, cc)

    square = jnp.zeros((8, TXT), F32)
    for j in range(8):
        both = jnp.concatenate([ts[j // 2, j % 2, 0].astype(F32), ts[j // 2, j % 2, 1].astype(F32)], axis=0)
        tt[j * 144 : (j + 1) * 144, :] = both.astype(BF16)
        square += jnp.sum((both * both).reshape(18, 8, TXT), axis=0)
    inv_txt = lax.rsqrt(jnp.sum(square, axis=0, keepdims=True) + EPS)
    inv_own[...] = jnp.broadcast_to(inv_txt, (8, TXT))

    @pl.when(is_home)
    def _():
        send(inv_own, inv_far, (inv_ss,), inv_rs, dev(c=cp), "home")

    row = lax.broadcasted_iota(jnp.int32, (SLAB, TXT), 0)
    col = lax.broadcasted_iota(jnp.int32, (SLAB, TXT), 1)
    side = (row >= HALF).astype(jnp.int32)
    rest = row - HALF * side
    gap = (rest >= 18).astype(jnp.int32) + (rest >= 36).astype(jnp.int32) + (rest >= 54).astype(jnp.int32)
    ahead = row + 504 * side + 18 * gap - col
    ahead += (x * 4 + zh * 2) * 576 + zb * 18 - (y * 8 + zm * 2 + c) * TXT
    loss_row = jnp.zeros((1, TXT), F32)
    inner = jnp.zeros((1, TXT), F32)

    def from_core(k, yy):
        arrived(ic_recv.at[yy], ic_rs.at[yy])
        total = iown[yy] + ic_recv[yy].astype(F32)
        if k < 3:
            iy_send[yy] = total.astype(BF16)
            send(iy_send.at[yy], iy_recv.at[y], (iy_ss, k), iy_rs.at[y], dev(y=yy))
        return total

    before = None
    for k, d in enumerate((2, 1, 3, 0)):
        yy = turn(y, d)
        arrived(xz.at[yy, cp], xc_rs.at[yy])
        for side_of in range(2):
            for q in range(4):
                first = side_of * HALF + q * ROWS
                xf[first : first + ROWS, :] = xz[yy, side_of, q].astype(F32)
        xs[yy] = xf[...].astype(BF16)
        slab = xs[yy]
        raw = dot(slab, tt[...], ((1,), (0,)))
        logits = raw * (sharpness * inv_txt) + offset
        diagonal = ahead == -144 * yy
        sign = jnp.where(diagonal, -1.0, 1.0)
        u = sign * logits
        e = jnp.exp(-jnp.abs(u))
        loss_row += jnp.sum(jnp.maximum(u, 0.0) + jnp.log1p(e), axis=0, keepdims=True)
        w = sign * (jnp.where(u >= 0, 1.0, e) / (1.0 + e)) * sharpness
        wb = w.astype(BF16)
        inner += jnp.sum(wb.astype(F32) * raw, axis=0, keepdims=True)
        w1[yy] = wb
        term[...] = dot((w * inv_txt).astype(BF16), tt[...], ((1,), (1,)))
        ic_send[yy] = term[pl.ds(pl.multiple_of(cp * HALF, 8), HALF), :].astype(BF16)
        send(ic_send.at[yy], ic_recv.at[yy], (ic_ss, k), ic_rs.at[yy], dev(c=cp))
        iown[yy] = term[pl.ds(pl.multiple_of(c * HALF, 8), HALF), :]
        if before is not None:
            from_core(*before)
        before = (k, yy)

    def loss_send(stage, place, others, value):
        ls[stage, place] = jnp.full((8, 128), value, F32)
        for k, peer in enumerate(others):
            send(ls.at[stage, place], ls.at[stage, place], (ls_ss, stage, k), ls_rs.at[stage, place], peer)

    def loss_wait(stage, places, n):
        for q in places:
            arrived(ls.at[stage, q], ls_rs.at[stage, q])
        total = ls[stage, 0]
        for q in range(1, n):
            total += ls[stage, q]
        return total

    loss_send(0, c, [dev(c=cp)], jnp.sum(loss_row))

    weights = w1[...].reshape(4 * SLAB, TXT)
    for q in range(3):
        part = xs[:, :, q * 384 : (q + 1) * 384].reshape(4 * SLAB, 384)
        dtf[q * 384 : (q + 1) * 384, :] = dot(part, weights, ((0,), (0,)))

    def features(xx, h, cc):
        return dtf[pl.ds(pl.multiple_of((xx * 4 + h * 2 + cc) * COLS, 8), COLS), :]

    for j, h in enumerate((zhp, zh)):
        for d in (2, 1, 3):
            xx = turn(x, d)
            for cc in range(2):
                tx_send[xx, h, cc] = pack(features(xx, h, cc), inner)
            send(tx_send.at[xx, h], tx_recv.at[x, h], (tx_ss, j, d - 1), tx_rs.at[x, h], dev(x=xx))

    total = from_core(*before)
    loss_v = loss_wait(0, [cp], 2)
    loss_send(1, y, [dev(y=turn(y, d)) for d in order], loss_v)
    for d in order:
        q = turn(y, d)
        arrived(iy_recv.at[q], iy_rs.at[q])
        total += iy_recv[q].astype(F32)
    xf[0:HALF, :] = total
    for q in range(4):
        iz_send[q] = xf[q * ROWS : (q + 1) * ROWS, :].astype(BF16)
    for k, d in enumerate((2, 1, 3)):
        q = turn(zm, d)
        send(iz_send.at[q], iz_recv.at[zm], (iz_ss, k), iz_rs.at[zm], dev(zm=q))
    loss_v = loss_wait(1, [turn(y, d) for d in order], 4)
    loss_send(2, zm, [dev(zm=turn(zm, d)) for d in order], loss_v)

    for j, h in enumerate((zhp, zh)):
        sums = [features(x, h, cc) for cc in range(2)]
        inn = inner
        for d in order:
            xx = turn(x, d)
            arrived(tx_recv.at[xx, h], tx_rs.at[xx, h])
            for cc in range(2):
                more, more_inn = unpack(tx_recv[xx, h, cc])
                sums[cc] += more
            inn += more_inn
        for cc in range(2):
            tacc[h, cc, 0:COLS] = sums[cc]
            tacc[h, cc, COLS:PIECE] = jnp.broadcast_to(inn, (8, TXT))

        @pl.when(is_guest)
        def _():
            for cc in range(2):
                tb_send[h, cc] = pack(tacc[h, cc, 0:COLS], tacc[h, cc, COLS : COLS + 1])
            send(tb_send.at[h], tb_recv.at[h], (tb_ss, j), tb_rs.at[h], dev(zb=zbp), "guest", lambda: tb_send.at[0])

    loss_v = loss_wait(2, [turn(zm, d) for d in order], 4)
    loss_send(3, x, [dev(x=turn(x, d)) for d in order], loss_v)

    @pl.when(is_home)
    def _():
        for h in (zhp, zh):
            arrived(tb_recv.at[h], tb_rs.at[h])
            for cc in range(2):
                more, more_inn = unpack(tb_recv[h, cc])
                data = tacc[h, cc, 0:COLS] + more
                inn = tacc[h, cc, COLS : COLS + 1] + more_inn
                tacc[h, cc, 0:COLS] = data
                tacc[h, cc, COLS:PIECE] = jnp.broadcast_to(inn, (8, TXT))
                if h is zhp:
                    tf_send[cc] = pack(data, inn)
                    send(tf_send.at[cc], tf_recv.at[1], (tf_ss, cc), tf_rs.at[1], dev(zh=zhp, c=cc), "home", lambda: tf_send.at[0])
        tf_send[2] = pack(tacc[zh, cp, 0:COLS], tacc[zh, cp, COLS : COLS + 1])
        send(tf_send.at[2], tf_recv.at[0], (tf_ss, 2), tf_rs.at[0], dev(c=cp), "home", lambda: tf_send.at[0])
        fin[...] = tacc[zh, c]

    loss_v = loss_wait(3, [turn(x, d) for d in order], 4)
    loss_send(4, zb, [dev(zb=zbp)], loss_v)

    total = iz_send[zm].astype(F32)
    for d in order:
        q = turn(zm, d)
        arrived(iz_recv.at[q], iz_rs.at[q])
        total += iz_recv[q].astype(F32)
    own_image = images[...].astype(F32)
    img_norm = lax.rsqrt(jnp.sum(own_image * own_image, axis=1, keepdims=True) + EPS)
    img_inner = jnp.sum(own_image * total, axis=1, keepdims=True)
    img_out[...] = img_norm * total - own_image * (img_norm * img_norm * img_norm * img_inner)
    loss_v = loss_wait(4, [zbp], 2)
    loss_send(5, zh, [dev(zh=zhp)], loss_v)

    @pl.when(is_guest)
    def _():
        arrived(inv_far, inv_rs)
        inv_own[...] = inv_far[...]
        arrived(tf_recv.at[0], tf_rs.at[0])
        data, inn = unpack(tf_recv[0])
        fin[0:COLS] = data
        fin[COLS:PIECE] = jnp.broadcast_to(inn, (8, TXT))

    arrived(tf_recv.at[1], tf_rs.at[1])
    more, more_inn = unpack(tf_recv[1])
    data = fin[0:COLS] + more
    inn = fin[COLS : COLS + 1] + more_inn
    norm = inv_own[0:1]
    txt_out[...] = norm * data - texts[...].astype(F32) * (norm * norm * norm * inn)
    loss_v = loss_wait(5, [zhp], 2)
    loss_out[0] = jnp.max(loss_v) / PAIRS

    sent("all")

    @pl.when(is_home)
    def _():
        sent("home")

    @pl.when(is_guest)
    def _():
        sent("guest")


def per_device(images, texts, logit_scale, bias):
    vmem = pl.BlockSpec(memory_space=pltpu.VMEM)
    smem = pl.BlockSpec(memory_space=pltpu.SMEM)
    sem = pltpu.SemaphoreType.DMA
    loss, grad_images, grad_texts = pl.pallas_call(
        kernel,
        out_shape=(
            jax.ShapeDtypeStruct((1,), F32),
            jax.ShapeDtypeStruct((ROWS, D), F32),
            jax.ShapeDtypeStruct((COLS, TXT), F32),
        ),
        in_specs=[vmem, vmem, smem, smem],
        out_specs=(smem, vmem, vmem),
        scratch_shapes=[
            pltpu.VMEM((4, 2, 4, ROWS, D), BF16),
            pltpu.VMEM((SLAB, D), F32),
            pltpu.VMEM((4, SLAB, D), BF16),
            pltpu.VMEM((4, 2, 2, COLS, TXT), BF16),
            pltpu.VMEM((D, TXT), BF16),
            pltpu.VMEM((8, TXT), F32),
            pltpu.VMEM((8, TXT), F32),
            pltpu.VMEM((4, SLAB, TXT), BF16),
            pltpu.VMEM((SLAB, D), F32),
            pltpu.VMEM((4, HALF, D), F32),
            pltpu.VMEM((4, HALF, D), BF16),
            pltpu.VMEM((4, HALF, D), BF16),
            pltpu.VMEM((4, HALF, D), BF16),
            pltpu.VMEM((4, HALF, D), BF16),
            pltpu.VMEM((4, ROWS, D), BF16),
            pltpu.VMEM((4, ROWS, D), BF16),
            pltpu.VMEM((D, TXT), F32),
            pltpu.VMEM((4, 2, 2, PIECE, TXT), BF16),
            pltpu.VMEM((4, 2, 2, PIECE, TXT), BF16),
            pltpu.VMEM((2, 2, PIECE, TXT), F32),
            pltpu.VMEM((2, 2, PIECE, TXT), BF16),
            pltpu.VMEM((2, 2, PIECE, TXT), BF16),
            pltpu.VMEM((3, PIECE, TXT), BF16),
            pltpu.VMEM((2, PIECE, TXT), BF16),
            pltpu.VMEM((PIECE, TXT), F32),
            pltpu.VMEM((6, 4, 8, 128), F32),
            sem((15,)), sem((4, 4)),
            sem((4,)), sem((4,)),
            sem((16,)), sem((4, 2, 2)),
            sem, sem,
            sem((4,)), sem((4,)),
            sem((3,)), sem((4,)),
            sem((3,)), sem((4,)),
            sem((2, 3)), sem((4, 2)),
            sem((2,)), sem((2,)),
            sem((3,)), sem((2,)),
            sem((6, 3)), sem((6, 4)),
        ],
        compiler_params=pltpu.CompilerParams(
            collective_id=0, has_side_effects=True, vmem_limit_bytes=48 * 1024 * 1024
        ),
        name="siglip",
    )(images, texts.T, logit_scale, bias)
    return loss, grad_images, grad_texts.T


def solution(mesh):
    return jax.shard_map(
        per_device,
        mesh=mesh,
        in_specs=(P(("img", "txt"), None), P("txt", "img"), P(), P()),
        out_specs=(P(), P(("img", "txt"), None), P("txt", "img")),
        check_vma=False,
    )
```

```python
import jax
import jax.numpy as jnp
from jax import lax
from jax.experimental import pallas as pl
from jax.experimental.pallas import tpu as pltpu
from jax.sharding import PartitionSpec as P

EPS = 1e-06
F32 = jnp.float32
BF16 = jnp.bfloat16
MESH = pl.DeviceIdType.MESH
D = 1152
PAIRS = 9216
ROWS = 18
HALF = 72
SLAB = 144
COLS = 72
TXT = 288
LANES = 384
DENSE = 168
PIECE = 176


def dot(a, b, dims):
    return lax.dot_general(a, b, (dims, ((), ())), preferred_element_type=F32)


def pack(data, inner):
    row = lax.broadcasted_iota(jnp.int32, (8, 128), 0)
    high = inner.astype(BF16).astype(F32)
    low = pltpu.roll(inner - high, 3, 0)
    tail = jnp.where(row < 3, high, jnp.where(row < 6, low, 0.0))
    return jnp.concatenate([data, tail], axis=0).astype(BF16)


def unpack(piece):
    wide = piece.astype(F32)
    tail = wide[DENSE:PIECE]
    return wide[:DENSE], tail + pltpu.roll(tail, 5, 0)


def densify(tiles):
    last = tiles[2]
    rest = last[0:24] + pltpu.roll(last[24:48], 32, 1) + pltpu.roll(last[48:72], 64, 1)
    return jnp.concatenate([tiles[0], tiles[1], rest], axis=0)


def last_tile(rest):
    lane = lax.broadcasted_iota(jnp.int32, (24, 128), 1)
    parts = [rest, pltpu.roll(rest, 96, 1), pltpu.roll(rest, 64, 1)]
    return jnp.concatenate([jnp.where(lane < 32, part, 0.0) for part in parts], axis=0)


def kernel(
    images, texts, scale, bias, loss_out, img_out, txt_out,
    xz, xf, xs, tp, tpad, ts, tt, inv_own, inv_far, w1, term, iown, ic_send, ic_recv, iy_send, iy_recv, iz_send, iz_recv,
    dtf, tx_send, tx_recv, tf_send, tf_recv, fin, ls,
    xz_ss, xz_rs, xc_ss, xc_rs, ts_ss, ts_rs, inv_ss, inv_rs, ic_ss, ic_rs, iy_ss, iy_rs, iz_ss, iz_rs,
    tx_ss, tx_rs, tf_ss, tf_rs, ls_ss, ls_rs,
):
    i = lax.axis_index("img")
    t = lax.axis_index("txt")
    x, zh, c = i // 4, (i // 2) % 2, i % 2
    y, zb, zm = t // 8, (t // 4) % 2, t % 4
    zbp, zhp, cp = 1 - zb, 1 - zh, 1 - c
    is_home = c == zb
    is_guest = c != zb

    def dev(x=x, zh=zh, c=c, y=y, zm=zm, zb=zb):
        return (x * 4 + zh * 2 + c, y * 8 + zb * 4 + zm)

    def turn(v, d):
        return lax.rem(v + d, 4)

    order = (1, 3, 2)
    peers = [dev(c=cp)]
    for cc in range(2):
        peers += [dev(zh=zhp, c=cc), dev(zb=zbp, c=cc), dev(zh=zhp, zb=zbp, c=cc)]
    for d in order:
        peers += [dev(x=turn(x, d)), dev(y=turn(y, d)), dev(zm=turn(zm, d))]
    barrier = pltpu.get_barrier_semaphore()
    for peer in peers:
        pl.semaphore_signal(barrier, inc=1, device_id=peer, device_id_type=MESH)

    pending = {"all": [], "home": [], "guest": []}

    def copy(src, dst, ss, rs, peer):
        return pltpu.make_async_remote_copy(
            src_ref=src, dst_ref=dst, send_sem=ss, recv_sem=rs, device_id=peer, device_id_type=MESH
        )

    def send(src, dst, ss, rs, peer, who="all", like=None):
        copy(src, dst, ss[0].at[ss[1:]] if ss[1:] else ss[0], rs, peer).start()
        pending[who].append((like or (lambda: src), ss))

    def sent(who):
        for like, ss in pending[who]:
            ref = like()
            copy(ref, ref, ss[0].at[ss[1:]] if ss[1:] else ss[0], ls_rs.at[0, 0], dev(c=cp)).wait_send()

    def arrived(ref, rs):
        copy(ref, ref, ls_ss.at[0, 0], rs, dev(c=cp)).wait_recv()

    sharpness = scale[0]
    offset = bias[0]

    own_image = images[...].astype(F32)
    img_norm = lax.rsqrt(jnp.sum(own_image * own_image, axis=1, keepdims=True) + EPS)
    xz[y, c, zm] = (own_image * img_norm).astype(BF16)
    tpad[...] = jnp.zeros((COLS, LANES), F32)
    tpad[:, 0:TXT] = texts[...].astype(F32)
    tp[...] = densify([tpad[:, j * 128 : (j + 1) * 128] for j in range(3)]).astype(BF16)

    pl.semaphore_wait(barrier, len(peers))

    counts = {"home": 0, "guest": 0}

    def t_send(who, xx, h, cc, peer, own=False):
        k = counts[who]
        counts[who] += 1
        slot = ts.at[xx, h, cc]
        send(tp if own else slot, slot, (ts_ss, k), ts_rs.at[xx, h, cc], peer, who, lambda: tp)

    def t_wait(xx, h, cc):
        arrived(ts.at[xx, h, cc], ts_rs.at[xx, h, cc])

    def t_over_x(who, h, cc, own=False):
        for d in (2, 1, 3):
            t_send(who, x, h, cc, dev(x=turn(x, d)), own)

    x_count = [0]

    def x_send(q, peer):
        k = x_count[0]
        x_count[0] += 1
        slot = xz.at[y, c, q]
        send(slot, slot, (xz_ss, k), xz_rs.at[y, q], peer)

    def x_wait(yy, q):
        arrived(xz.at[yy, c, q], xz_rs.at[yy, q])

    def x_over_y(q):
        for d in (2, 1, 3):
            x_send(q, dev(y=turn(y, d)))

    def x_to_core(k, yy):
        group = xz.at[yy, c]
        send(group, group, (xc_ss, k), xc_rs.at[yy], dev(c=cp))

    @pl.when(is_home)
    def _():
        t_send("home", x, zh, c, dev(zb=zbp), True)
        t_send("home", x, zh, c, dev(zh=zhp, zb=zbp), True)
        t_over_x("home", zh, c, True)
        ts[x, zh, c] = tp[...]

    @pl.when(is_guest)
    def _():
        t_send("guest", x, zh, c, dev(zb=zbp, c=cp), True)
        t_send("guest", x, zh, c, dev(zh=zhp, zb=zbp, c=cp), True)
        t_send("guest", x, zh, c, dev(c=cp), True)

    for d in (1, 3, 2):
        x_send(zm, dev(zm=turn(zm, d)))
    x_over_y(zm)

    @pl.when(is_home)
    def _():
        t_wait(x, zh, cp)
        t_over_x("home", zh, cp)

    @pl.when(is_guest)
    def _():
        for h in (zh, zhp):
            t_wait(x, h, zh)
            t_send("guest", x, h, zh, dev(zh=1 - h, zb=zbp))
            t_over_x("guest", h, zh)

    for d in order:
        x_wait(y, turn(zm, d))
        x_over_y(turn(zm, d))
    x_to_core(0, y)

    @pl.when(is_guest)
    def _():
        for h in (zh, zhp):
            t_wait(x, h, zhp)
            t_over_x("guest", h, zhp)

    @pl.when(is_home)
    def _():
        for cc in range(2):
            t_wait(x, zhp, cc)
            t_over_x("home", zhp, cc)

    for d in order:
        yy = turn(y, d)
        for q in range(4):
            x_wait(yy, turn(zm, q))
        x_to_core(d, yy)
    for h in (zh, zhp):
        for cc in range(2):
            for d in order:
                t_wait(turn(x, d), h, cc)

    square = jnp.zeros((8, LANES), F32)
    for j in range(8):
        halves = []
        for cc in range(2):
            block = ts[j // 2, j % 2, cc].astype(F32)
            halves.append(jnp.concatenate([block[0:72], block[72:144], last_tile(block[144:DENSE])], axis=1))
        both = jnp.concatenate(halves, axis=0)
        tt[j * 144 : (j + 1) * 144, :] = both.astype(BF16)
        square += jnp.sum((both * both).reshape(18, 8, LANES), axis=0)
    inv_txt = lax.rsqrt(jnp.sum(square, axis=0, keepdims=True) + EPS)
    inv_own[...] = jnp.broadcast_to(inv_txt, (8, LANES))

    @pl.when(is_home)
    def _():
        send(inv_own, inv_far, (inv_ss,), inv_rs, dev(c=cp), "home")

    row = lax.broadcasted_iota(jnp.int32, (SLAB, LANES), 0)
    col = lax.broadcasted_iota(jnp.int32, (SLAB, LANES), 1)
    side = (row >= HALF).astype(jnp.int32)
    ahead = row + 504 * side - col + (x * 4 + zh * 2) * 576 + zb * 72 - (y * 8 + c * 4 + zm) * TXT
    valid = col < TXT
    loss_row = jnp.zeros((1, LANES), F32)
    inner = jnp.zeros((1, LANES), F32)

    def from_core(k, yy):
        arrived(ic_recv.at[yy], ic_rs.at[yy])
        total = iown[yy] + ic_recv[yy].astype(F32)
        if k < 3:
            iy_send[yy] = total.astype(BF16)
            send(iy_send.at[yy], iy_recv.at[y], (iy_ss, k), iy_rs.at[y], dev(y=yy))
        return total

    before = None
    for k, d in enumerate((2, 1, 3, 0)):
        yy = turn(y, d)
        arrived(xz.at[yy, cp], xc_rs.at[yy])
        for side_of in range(2):
            for q in range(4):
                first = side_of * HALF + q * ROWS
                xf[first : first + ROWS, :] = xz[yy, side_of, q].astype(F32)
        xs[yy] = xf[...].astype(BF16)
        slab = xs[yy]
        raw = dot(slab, tt[...], ((1,), (0,)))
        logits = raw * (sharpness * inv_txt) + offset
        diagonal = ahead == -144 * yy
        sign = jnp.where(diagonal, -1.0, 1.0)
        u = sign * logits
        e = jnp.exp(-jnp.abs(u))
        soft = jnp.maximum(u, 0.0) + jnp.log1p(e)
        loss_row += jnp.sum(jnp.where(valid, soft, 0.0), axis=0, keepdims=True)
        w = sign * (jnp.where(u >= 0, 1.0, e) / (1.0 + e)) * sharpness
        w = jnp.where(valid, w, 0.0)
        wb = w.astype(BF16)
        inner += jnp.sum(wb.astype(F32) * raw, axis=0, keepdims=True)
        w1[yy] = wb
        term[...] = dot((w * inv_txt).astype(BF16), tt[...], ((1,), (1,)))
        ic_send[yy] = term[pl.ds(pl.multiple_of(cp * HALF, 8), HALF), :].astype(BF16)
        send(ic_send.at[yy], ic_recv.at[yy], (ic_ss, k), ic_rs.at[yy], dev(c=cp))
        iown[yy] = term[pl.ds(pl.multiple_of(c * HALF, 8), HALF), :]
        if before is not None:
            from_core(*before)
        before = (k, yy)

    def loss_send(stage, place, others, value):
        ls[stage, place] = jnp.full((8, 128), value, F32)
        for k, peer in enumerate(others):
            send(ls.at[stage, place], ls.at[stage, place], (ls_ss, stage, k), ls_rs.at[stage, place], peer)

    def loss_wait(stage, places, n):
        for q in places:
            arrived(ls.at[stage, q], ls_rs.at[stage, q])
        total = ls[stage, 0]
        for q in range(1, n):
            total += ls[stage, q]
        return total

    loss_send(0, c, [dev(c=cp)], jnp.sum(loss_row))

    weights = w1[...].reshape(4 * SLAB, LANES)
    for q in range(3):
        part = xs[:, :, q * 384 : (q + 1) * 384].reshape(4 * SLAB, 384)
        dtf[q * 384 : (q + 1) * 384, :] = dot(part, weights, ((0,), (0,)))

    inner_tile = jnp.concatenate([inner[:, j * 128 : (j + 1) * 128] for j in range(3)] + [jnp.zeros((5, 128), F32)], axis=0)

    def features(xx, h, cc):
        rows = pl.ds(pl.multiple_of((xx * 4 + h * 2 + cc) * COLS, 8), COLS)
        return densify([dtf[rows, j * 128 : (j + 1) * 128] for j in range(3)])

    for j, h in enumerate((zhp, zh)):
        for d in (2, 1, 3):
            xx = turn(x, d)
            for cc in range(2):
                tx_send[xx, h, cc] = pack(features(xx, h, cc), inner_tile)
            send(tx_send.at[xx, h], tx_recv.at[x, h], (tx_ss, j, d - 1), tx_rs.at[x, h], dev(x=xx))

    total = from_core(*before)
    loss_v = loss_wait(0, [cp], 2)
    loss_send(1, zh * 2 + zb, [dev(zh=zhp), dev(zb=zbp), dev(zh=zhp, zb=zbp)], loss_v)
    for d in order:
        q = turn(y, d)
        arrived(iy_recv.at[q], iy_rs.at[q])
        total += iy_recv[q].astype(F32)
    xf[0:HALF, :] = total
    for q in range(4):
        iz_send[q] = xf[q * ROWS : (q + 1) * ROWS, :].astype(BF16)
    for k, d in enumerate((2, 1, 3)):
        q = turn(zm, d)
        send(iz_send.at[q], iz_recv.at[zm], (iz_ss, k), iz_rs.at[zm], dev(zm=q))
    loss_v = loss_wait(1, [zhp * 2 + zb, zh * 2 + zbp, zhp * 2 + zbp], 4)
    loss_send(2, y, [dev(y=turn(y, d)) for d in order], loss_v)

    for j, h in enumerate((zhp, zh)):
        sums = [features(x, h, cc) for cc in range(2)]
        inn = inner_tile
        for d in order:
            xx = turn(x, d)
            arrived(tx_recv.at[xx, h], tx_rs.at[xx, h])
            for cc in range(2):
                more, more_inn = unpack(tx_recv[xx, h, cc])
                sums[cc] += more
            inn += more_inn
        for cc in range(2):
            tf_send[j, cc] = pack(sums[cc], inn)

        @pl.when(is_guest)
        def _():
            for cc in range(2):
                send(tf_send.at[j, cc], tf_recv.at[zh, zb], (tf_ss, j, cc), tf_rs.at[zh, zb], dev(zh=h, zb=zbp, c=cc),
                     "guest", lambda: tf_send.at[0, 0])

        @pl.when(is_home)
        def _():
            if j == 0:
                for cc in range(2):
                    send(tf_send.at[j, cc], tf_recv.at[zh, zb], (tf_ss, j, cc), tf_rs.at[zh, zb], dev(zh=h, c=cc),
                         "home", lambda: tf_send.at[0, 0])
            else:
                send(tf_send.at[j, cp], tf_recv.at[zh, zb], (tf_ss, j, 0), tf_rs.at[zh, zb], dev(c=cp),
                     "home", lambda: tf_send.at[0, 0])
                for cc in range(2):
                    @pl.when(c == cc)
                    def _():
                        fin[0:DENSE] = sums[cc]
                        fin[DENSE:PIECE] = inn

        if j == 0:
            loss_v = loss_wait(2, [turn(y, d) for d in order], 4)
            loss_send(3, zm, [dev(zm=turn(zm, d)) for d in order], loss_v)

    total = iz_send[zm].astype(F32)
    for d in order:
        q = turn(zm, d)
        arrived(iz_recv.at[q], iz_rs.at[q])
        total += iz_recv[q].astype(F32)
    own_image = images[...].astype(F32)
    img_norm = lax.rsqrt(jnp.sum(own_image * own_image, axis=1, keepdims=True) + EPS)
    img_inner = jnp.sum(own_image * total, axis=1, keepdims=True)
    img_out[...] = img_norm * total - own_image * (img_norm * img_norm * img_norm * img_inner)
    loss_v = loss_wait(3, [turn(zm, d) for d in order], 4)
    loss_send(4, x, [dev(x=turn(x, d)) for d in order], loss_v)

    @pl.when(is_guest)
    def _():
        arrived(inv_far, inv_rs)
        inv_own[...] = inv_far[...]
        arrived(tf_recv.at[zh, zb], tf_rs.at[zh, zb])
        data, inn = unpack(tf_recv[zh, zb])
        fin[0:DENSE] = data
        fin[DENSE:PIECE] = inn

    data = fin[0:DENSE]
    inn = fin[DENSE:PIECE]
    for h, b in ((zh, zbp), (zhp, zbp), (zhp, zb)):
        arrived(tf_recv.at[h, b], tf_rs.at[h, b])
        more, more_inn = unpack(tf_recv[h, b])
        data += more
        inn += more_inn
    columns = (data[0:72], data[72:144], last_tile(data[144:DENSE]))
    for j in range(3):
        norm = inv_own[0:1, j * 128 : (j + 1) * 128]
        tpad[:, j * 128 : (j + 1) * 128] = norm * columns[j] - tpad[:, j * 128 : (j + 1) * 128] * (
            norm * norm * norm * inn[j : j + 1]
        )
    txt_out[...] = tpad[:, 0:TXT]
    loss_v = loss_wait(4, [turn(x, d) for d in order], 4)
    loss_out[0] = jnp.max(loss_v) / PAIRS

    sent("all")

    @pl.when(is_home)
    def _():
        sent("home")

    @pl.when(is_guest)
    def _():
        sent("guest")


def per_device(images, texts, logit_scale, bias):
    vmem = pl.BlockSpec(memory_space=pltpu.VMEM)
    smem = pl.BlockSpec(memory_space=pltpu.SMEM)
    sem = pltpu.SemaphoreType.DMA
    loss, grad_images, grad_texts = pl.pallas_call(
        kernel,
        out_shape=(
            jax.ShapeDtypeStruct((1,), F32),
            jax.ShapeDtypeStruct((ROWS, D), F32),
            jax.ShapeDtypeStruct((COLS, TXT), F32),
        ),
        in_specs=[vmem, vmem, smem, smem],
        out_specs=(smem, vmem, vmem),
        scratch_shapes=[
            pltpu.VMEM((4, 2, 4, ROWS, D), BF16),
            pltpu.VMEM((SLAB, D), F32),
            pltpu.VMEM((4, SLAB, D), BF16),
            pltpu.VMEM((DENSE, 128), BF16),
            pltpu.VMEM((COLS, LANES), F32),
            pltpu.VMEM((4, 2, 2, DENSE, 128), BF16),
            pltpu.VMEM((D, LANES), BF16),
            pltpu.VMEM((8, LANES), F32),
            pltpu.VMEM((8, LANES), F32),
            pltpu.VMEM((4, SLAB, LANES), BF16),
            pltpu.VMEM((SLAB, D), F32),
            pltpu.VMEM((4, HALF, D), F32),
            pltpu.VMEM((4, HALF, D), BF16),
            pltpu.VMEM((4, HALF, D), BF16),
            pltpu.VMEM((4, HALF, D), BF16),
            pltpu.VMEM((4, HALF, D), BF16),
            pltpu.VMEM((4, ROWS, D), BF16),
            pltpu.VMEM((4, ROWS, D), BF16),
            pltpu.VMEM((D, LANES), F32),
            pltpu.VMEM((4, 2, 2, PIECE, 128), BF16),
            pltpu.VMEM((4, 2, 2, PIECE, 128), BF16),
            pltpu.VMEM((2, 2, PIECE, 128), BF16),
            pltpu.VMEM((2, 2, PIECE, 128), BF16),
            pltpu.VMEM((PIECE, 128), F32),
            pltpu.VMEM((5, 4, 8, 128), F32),
            sem((15,)), sem((4, 4)),
            sem((4,)), sem((4,)),
            sem((17,)), sem((4, 2, 2)),
            sem, sem,
            sem((4,)), sem((4,)),
            sem((3,)), sem((4,)),
            sem((3,)), sem((4,)),
            sem((2, 3)), sem((4, 2)),
            sem((2, 2)), sem((2, 2)),
            sem((5, 3)), sem((5, 4)),
        ],
        compiler_params=pltpu.CompilerParams(
            collective_id=0, has_side_effects=True, vmem_limit_bytes=48 * 1024 * 1024
        ),
        name="siglip",
    )(images, texts.T, logit_scale, bias)
    return loss, grad_images, grad_texts.T


def solution(mesh):
    return jax.shard_map(
        per_device,
        mesh=mesh,
        in_specs=(P(("img", "txt"), None), P("txt", "img"), P(), P()),
        out_specs=(P(), P(("img", "txt"), None), P("txt", "img")),
        check_vma=False,
    )
```

```python
import jax
import jax.numpy as jnp
from jax import lax
from jax.experimental import pallas as pl
from jax.experimental.pallas import tpu as pltpu
from jax.sharding import PartitionSpec as P

EPS = 1e-06
F32 = jnp.float32
BF16 = jnp.bfloat16
MESH = pl.DeviceIdType.MESH
D = 1152
PAIRS = 9216
ROWS = 18
HALF = 72
SLAB = 144
COLS = 72
TXT = 288
LANES = 384
DENSE = 168
PIECE = 176


def dot(a, b, dims):
    return lax.dot_general(a, b, (dims, ((), ())), preferred_element_type=F32)


def pack(data, inner):
    row = lax.broadcasted_iota(jnp.int32, (8, 128), 0)
    high = inner.astype(BF16).astype(F32)
    low = pltpu.roll(inner - high, 3, 0)
    tail = jnp.where(row < 3, high, jnp.where(row < 6, low, 0.0))
    return jnp.concatenate([data, tail], axis=0).astype(BF16)


def unpack(piece):
    wide = piece.astype(F32)
    tail = wide[DENSE:PIECE]
    return wide[:DENSE], tail + pltpu.roll(tail, 5, 0)


def densify(tiles):
    last = tiles[2]
    rest = last[0:24] + pltpu.roll(last[24:48], 32, 1) + pltpu.roll(last[48:72], 64, 1)
    return jnp.concatenate([tiles[0], tiles[1], rest], axis=0)


def last_tile(rest):
    lane = lax.broadcasted_iota(jnp.int32, (24, 128), 1)
    parts = [rest, pltpu.roll(rest, 96, 1), pltpu.roll(rest, 64, 1)]
    return jnp.concatenate([jnp.where(lane < 32, part, 0.0) for part in parts], axis=0)


def kernel(
    images, texts, scale, bias, loss_out, img_out, txt_out,
    xz, xf, xs, tp, tpad, ts, tt, inv_own, inv_far, w1, w2, term, iown, ic_send, ic_recv, iy_send, iy_recv, iz_send, iz_recv,
    dtf, tx_send, tx_recv, tf_send, tf_recv, tg_recv, tsum, fin, ls,
    xz_ss, xz_rs, xc_ss, xc_rs, ts_ss, ts_rs, inv_ss, inv_rs, ic_ss, ic_rs, iy_ss, iy_rs, iz_ss, iz_rs,
    tx_ss, tx_rs, tf_ss, tf_rs, tg_rs, ls_ss, ls_rs,
):
    i = lax.axis_index("img")
    t = lax.axis_index("txt")
    x, zh, c = i // 4, (i // 2) % 2, i % 2
    y, zb, zm = t // 8, (t // 4) % 2, t % 4
    zbp, zhp, cp = 1 - zb, 1 - zh, 1 - c
    is_home = c == zb
    is_guest = c != zb

    def dev(x=x, zh=zh, c=c, y=y, zm=zm, zb=zb):
        return (x * 4 + zh * 2 + c, y * 8 + zb * 4 + zm)

    def turn(v, d):
        return lax.rem(v + d, 4)

    order = (1, 3, 2)
    peers = [dev(c=cp)]
    for cc in range(2):
        peers += [dev(zh=zhp, c=cc), dev(zb=zbp, c=cc), dev(zh=zhp, zb=zbp, c=cc)]
    for d in order:
        peers += [dev(x=turn(x, d)), dev(y=turn(y, d)), dev(zm=turn(zm, d))]
    barrier = pltpu.get_barrier_semaphore()
    for peer in peers:
        pl.semaphore_signal(barrier, inc=1, device_id=peer, device_id_type=MESH)

    pending = {"all": [], "home": [], "guest": []}

    def copy(src, dst, ss, rs, peer):
        return pltpu.make_async_remote_copy(
            src_ref=src, dst_ref=dst, send_sem=ss, recv_sem=rs, device_id=peer, device_id_type=MESH
        )

    def send(src, dst, ss, rs, peer, who="all", like=None):
        copy(src, dst, ss[0].at[ss[1:]] if ss[1:] else ss[0], rs, peer).start()
        pending[who].append((like or (lambda: src), ss))

    def sent(who):
        for like, ss in pending[who]:
            ref = like()
            copy(ref, ref, ss[0].at[ss[1:]] if ss[1:] else ss[0], ls_rs.at[0, 0], dev(c=cp)).wait_send()

    def arrived(ref, rs):
        copy(ref, ref, ls_ss.at[0, 0], rs, dev(c=cp)).wait_recv()

    sharpness = scale[0]
    offset = bias[0]

    own_image = images[...].astype(F32)
    img_norm = lax.rsqrt(jnp.sum(own_image * own_image, axis=1, keepdims=True) + EPS)
    xz[y, c, zm] = (own_image * img_norm).astype(BF16)
    tpad[...] = jnp.zeros((COLS, LANES), F32)
    tpad[:, 0:TXT] = texts[...].astype(F32)
    tp[...] = densify([tpad[:, j * 128 : (j + 1) * 128] for j in range(3)]).astype(BF16)

    pl.semaphore_wait(barrier, len(peers))

    counts = {"home": 0, "guest": 0}

    def t_send(who, xx, h, cc, peer, own=False):
        k = counts[who]
        counts[who] += 1
        slot = ts.at[xx, h, cc]
        send(tp if own else slot, slot, (ts_ss, k), ts_rs.at[xx, h, cc], peer, who, lambda: tp)

    def t_wait(xx, h, cc):
        arrived(ts.at[xx, h, cc], ts_rs.at[xx, h, cc])

    def t_over_x(who, h, cc, own=False):
        for d in (2, 1, 3):
            t_send(who, x, h, cc, dev(x=turn(x, d)), own)

    x_count = [0]

    def x_send(q, peer):
        k = x_count[0]
        x_count[0] += 1
        slot = xz.at[y, c, q]
        send(slot, slot, (xz_ss, k), xz_rs.at[y, q], peer)

    def x_wait(yy, q):
        arrived(xz.at[yy, c, q], xz_rs.at[yy, q])

    def x_over_y(q):
        for d in (2, 1, 3):
            x_send(q, dev(y=turn(y, d)))

    def x_to_core(k, yy):
        group = xz.at[yy, c]
        send(group, group, (xc_ss, k), xc_rs.at[yy], dev(c=cp))

    @pl.when(is_home)
    def _():
        t_send("home", x, zh, c, dev(zb=zbp), True)
        t_send("home", x, zh, c, dev(zh=zhp, zb=zbp), True)
        t_over_x("home", zh, c, True)
        ts[x, zh, c] = tp[...]

    @pl.when(is_guest)
    def _():
        t_send("guest", x, zh, c, dev(zb=zbp, c=cp), True)
        t_send("guest", x, zh, c, dev(zh=zhp, zb=zbp, c=cp), True)
        t_send("guest", x, zh, c, dev(c=cp), True)

    x_over_y(zm)
    for who in ("home", "guest"):
        pending[who] = pending[who][2:]
    for k in range(2):
        copy(tp, tp, ts_ss.at[k], ls_rs.at[0, 0], dev(c=cp)).wait_send()
    for d in (1, 3, 2):
        x_send(zm, dev(zm=turn(zm, d)))

    @pl.when(is_home)
    def _():
        t_wait(x, zh, cp)
        t_over_x("home", zh, cp)

    @pl.when(is_guest)
    def _():
        for h in (zh, zhp):
            t_wait(x, h, zh)
            t_send("guest", x, h, zh, dev(zh=1 - h, zb=zbp))
            t_over_x("guest", h, zh)

    for d in order:
        x_wait(y, turn(zm, d))
        x_over_y(turn(zm, d))
    x_to_core(0, y)

    @pl.when(is_guest)
    def _():
        for h in (zh, zhp):
            t_wait(x, h, zhp)
            t_over_x("guest", h, zhp)

    @pl.when(is_home)
    def _():
        for cc in range(2):
            t_wait(x, zhp, cc)
            t_over_x("home", zhp, cc)

    for d in order:
        yy = turn(y, d)
        for q in range(4):
            x_wait(yy, turn(zm, q))
        x_to_core(d, yy)
    for d in (0, 1, 3, 2):
        yy = turn(y, d)
        arrived(xz.at[yy, cp], xc_rs.at[yy])
        for side_of in range(2):
            for q in range(4):
                first = side_of * HALF + q * ROWS
                xf[first : first + ROWS, :] = xz[yy, side_of, q].astype(F32)
        xs[yy] = xf[...].astype(BF16)

    square = jnp.zeros((8, LANES), F32)
    for h in (zh, zhp):
        for d in (0, 1, 3, 2):
            xx = turn(x, d)
            halves = []
            for cc in range(2):
                if d:
                    t_wait(xx, h, cc)
                block = ts[xx, h, cc].astype(F32)
                halves.append(jnp.concatenate([block[0:72], block[72:144], last_tile(block[144:DENSE])], axis=1))
            both = jnp.concatenate(halves, axis=0)
            tt[pl.ds(pl.multiple_of((xx * 2 + h) * 144, 16), 144), :] = both.astype(BF16)
            square += jnp.sum((both * both).reshape(18, 8, LANES), axis=0)
    inv_txt = lax.rsqrt(jnp.sum(square, axis=0, keepdims=True) + EPS)
    inv_own[...] = jnp.broadcast_to(inv_txt, (8, LANES))

    @pl.when(is_home)
    def _():
        send(inv_own, inv_far, (inv_ss,), inv_rs, dev(c=cp), "home")

    row = lax.broadcasted_iota(jnp.int32, (SLAB, LANES), 0)
    col = lax.broadcasted_iota(jnp.int32, (SLAB, LANES), 1)
    side = (row >= HALF).astype(jnp.int32)
    ahead = row + 504 * side - col + (x * 4 + zh * 2) * 576 + zb * 72 - (y * 8 + c * 4 + zm) * TXT
    valid = col < TXT
    loss_row = jnp.zeros((1, LANES), F32)
    inner = jnp.zeros((1, LANES), F32)

    for d in (0, 1, 3, 2):
        yy = turn(y, d)
        slab = xs[yy]
        raw = dot(slab, tt[...], ((1,), (0,)))
        logits = raw * (sharpness * inv_txt) + offset
        diagonal = ahead == -144 * yy
        sign = jnp.where(diagonal, -1.0, 1.0)
        u = sign * logits
        e = jnp.exp(-jnp.abs(u))
        soft = jnp.maximum(u, 0.0) + jnp.log1p(e)
        loss_row += jnp.sum(jnp.where(valid, soft, 0.0), axis=0, keepdims=True)
        w = sign * (jnp.where(u >= 0, 1.0, e) / (1.0 + e)) * sharpness
        w = jnp.where(valid, w, 0.0)
        wb = w.astype(BF16)
        inner += jnp.sum(wb.astype(F32) * raw, axis=0, keepdims=True)
        w1[yy] = wb
        w2[yy] = (w * inv_txt).astype(BF16)

    def loss_send(stage, place, others, value):
        ls[stage, place] = jnp.full((8, 128), value, F32)
        for k, peer in enumerate(others):
            send(ls.at[stage, place], ls.at[stage, place], (ls_ss, stage, k), ls_rs.at[stage, place], peer)

    def loss_wait(stage, places, n):
        for q in places:
            arrived(ls.at[stage, q], ls_rs.at[stage, q])
        total = ls[stage, 0]
        for q in range(1, n):
            total += ls[stage, q]
        return total

    loss_send(0, c, [dev(c=cp)], jnp.sum(loss_row))

    weights = w1[...].reshape(4 * SLAB, LANES)
    for q in range(3):
        part = xs[:, :, q * 384 : (q + 1) * 384].reshape(4 * SLAB, 384)
        dtf[q * 384 : (q + 1) * 384, :] = dot(part, weights, ((0,), (0,)))

    inner_tile = jnp.concatenate([inner[:, j * 128 : (j + 1) * 128] for j in range(3)] + [jnp.zeros((5, 128), F32)], axis=0)

    def features(xx, h, cc):
        rows = pl.ds(pl.multiple_of((xx * 4 + h * 2 + cc) * COLS, 8), COLS)
        return densify([dtf[rows, j * 128 : (j + 1) * 128] for j in range(3)])

    def which(j, m):
        h = jnp.where(is_home, (zhp, zh)[j], m)
        cc = jnp.where(is_home, m, (1 - zh, zh)[j])
        return h, cc

    for j in range(2):
        for d in (2, 1, 3):
            xx = turn(x, d)
            for m in range(2):
                tx_send[xx, j, m] = pack(features(xx, *which(j, m)), inner_tile)
            send(tx_send.at[xx, j], tx_recv.at[x, j], (tx_ss, j, d - 1), tx_rs.at[x, j], dev(x=xx))

    def from_core(k, yy):
        arrived(ic_recv.at[yy], ic_rs.at[yy])
        total = iown[yy] + ic_recv[yy].astype(F32)
        if k < 3:
            iy_send[yy] = total.astype(BF16)
            send(iy_send.at[yy], iy_recv.at[y], (iy_ss, k), iy_rs.at[y], dev(y=yy))
        return total

    before = None
    for k, d in enumerate((2, 1, 3, 0)):
        yy = turn(y, d)
        term[...] = dot(w2[yy], tt[...], ((1,), (1,)))
        ic_send[yy] = term[pl.ds(pl.multiple_of(cp * HALF, 8), HALF), :].astype(BF16)
        send(ic_send.at[yy], ic_recv.at[yy], (ic_ss, k), ic_rs.at[yy], dev(c=cp))
        iown[yy] = term[pl.ds(pl.multiple_of(c * HALF, 8), HALF), :]
        if before is not None:
            from_core(*before)
        before = (k, yy)

    total = from_core(*before)
    loss_v = loss_wait(0, [cp], 2)
    loss_send(1, zh * 2 + zb, [dev(zh=zhp), dev(zb=zbp), dev(zh=zhp, zb=zbp)], loss_v)
    def to_owners(j):
        sums = [features(x, *which(j, m)) for m in range(2)]
        inn = inner_tile
        for d in order:
            xx = turn(x, d)
            arrived(tx_recv.at[xx, j], tx_rs.at[xx, j])
            for m in range(2):
                more, more_inn = unpack(tx_recv[xx, j, m])
                sums[m] += more
            inn += more_inn
        if j == 0:
            for m in range(2):
                tf_send[0, m] = pack(sums[m], inn)

            @pl.when(is_home)
            def _():
                for m in range(2):
                    send(tf_send.at[0, m], tg_recv.at[zh], (tf_ss, 0, m), tg_rs.at[zh], dev(zh=m, zb=zbp),
                         "home", lambda: tf_send.at[0, 0])

            @pl.when(is_guest)
            def _():
                for m in range(2):
                    send(tf_send.at[0, m], tf_recv.at[zh], (tf_ss, 0, m), tf_rs.at[zh, 0], dev(zh=m, zb=zbp, c=1 - zh),
                         "guest", lambda: tf_send.at[0, 0])
        else:
            for m in range(2):
                tsum[m, 0:DENSE] = sums[m]
                tsum[m, DENSE:PIECE] = inn

            @pl.when(is_home)
            def _():
                tf_send[1, 0] = pack(tsum[cp, 0:DENSE], tsum[cp, DENSE:PIECE])
                send(tf_send.at[1, 0], tf_recv.at[2], (tf_ss, 1, 0), tf_rs.at[0, 1], dev(c=cp),
                     "home", lambda: tf_send.at[0, 0])
                fin[...] = tsum[c]

            @pl.when(is_guest)
            def _():
                for m in range(2):
                    arrived(tg_recv.at[1 - m], tg_rs.at[1 - m])
                    more, more_inn = unpack(tg_recv[1 - m])
                    tf_send[1, m] = pack(tsum[m, 0:DENSE] + more, tsum[m, DENSE:PIECE] + more_inn)
                    send(tf_send.at[1, m], tf_recv.at[zh], (tf_ss, 1, m), tf_rs.at[zh, 0], dev(zh=m, zb=zbp, c=zh),
                         "guest", lambda: tf_send.at[0, 0])

    to_owners(0)
    for d in order:
        q = turn(y, d)
        arrived(iy_recv.at[q], iy_rs.at[q])
        total += iy_recv[q].astype(F32)
    xf[0:HALF, :] = total
    for q in range(4):
        iz_send[q] = xf[q * ROWS : (q + 1) * ROWS, :].astype(BF16)
    for k, d in enumerate((2, 1, 3)):
        q = turn(zm, d)
        send(iz_send.at[q], iz_recv.at[zm], (iz_ss, k), iz_rs.at[zm], dev(zm=q))
    loss_v = loss_wait(1, [zhp * 2 + zb, zh * 2 + zbp, zhp * 2 + zbp], 4)
    loss_send(2, y, [dev(y=turn(y, d)) for d in order], loss_v)

    to_owners(1)
    loss_v = loss_wait(2, [turn(y, d) for d in order], 4)
    loss_send(3, zm, [dev(zm=turn(zm, d)) for d in order], loss_v)

    total = iz_send[zm].astype(F32)
    for d in order:
        q = turn(zm, d)
        arrived(iz_recv.at[q], iz_rs.at[q])
        total += iz_recv[q].astype(F32)
    own_image = images[...].astype(F32)
    img_norm = lax.rsqrt(jnp.sum(own_image * own_image, axis=1, keepdims=True) + EPS)
    img_inner = jnp.sum(own_image * total, axis=1, keepdims=True)
    img_out[...] = img_norm * total - own_image * (img_norm * img_norm * img_norm * img_inner)
    loss_v = loss_wait(3, [turn(zm, d) for d in order], 4)
    loss_send(4, x, [dev(x=turn(x, d)) for d in order], loss_v)

    @pl.when(is_guest)
    def _():
        arrived(inv_far, inv_rs)
        inv_own[...] = inv_far[...]
        arrived(tf_recv.at[2], tf_rs.at[0, 1])
        data, inn = unpack(tf_recv[2])
        fin[0:DENSE] = data
        fin[DENSE:PIECE] = inn

    data = fin[0:DENSE]
    inn = fin[DENSE:PIECE]
    for g in (1 - c, c):
        arrived(tf_recv.at[g], tf_rs.at[g, 0])
        more, more_inn = unpack(tf_recv[g])
        data += more
        inn += more_inn
    columns = (data[0:72], data[72:144], last_tile(data[144:DENSE]))
    for j in range(3):
        norm = inv_own[0:1, j * 128 : (j + 1) * 128]
        tpad[:, j * 128 : (j + 1) * 128] = norm * columns[j] - tpad[:, j * 128 : (j + 1) * 128] * (
            norm * norm * norm * inn[j : j + 1]
        )
    txt_out[...] = tpad[:, 0:TXT]
    loss_v = loss_wait(4, [turn(x, d) for d in order], 4)
    loss_out[...] = loss_v / PAIRS

    sent("all")

    @pl.when(is_home)
    def _():
        sent("home")

    @pl.when(is_guest)
    def _():
        sent("guest")


def per_device(images, texts, logit_scale, bias):
    vmem = pl.BlockSpec(memory_space=pltpu.VMEM)
    smem = pl.BlockSpec(memory_space=pltpu.SMEM)
    sem = pltpu.SemaphoreType.DMA
    loss, grad_images, grad_texts = pl.pallas_call(
        kernel,
        out_shape=(
            jax.ShapeDtypeStruct((8, 128), F32),
            jax.ShapeDtypeStruct((ROWS, D), F32),
            jax.ShapeDtypeStruct((COLS, TXT), F32),
        ),
        in_specs=[vmem, vmem, smem, smem],
        out_specs=(vmem, vmem, vmem),
        scratch_shapes=[
            pltpu.VMEM((4, 2, 4, ROWS, D), BF16),
            pltpu.VMEM((SLAB, D), F32),
            pltpu.VMEM((4, SLAB, D), BF16),
            pltpu.VMEM((DENSE, 128), BF16),
            pltpu.VMEM((COLS, LANES), F32),
            pltpu.VMEM((4, 2, 2, DENSE, 128), BF16),
            pltpu.VMEM((D, LANES), BF16),
            pltpu.VMEM((8, LANES), F32),
            pltpu.VMEM((8, LANES), F32),
            pltpu.VMEM((4, SLAB, LANES), BF16),
            pltpu.VMEM((4, SLAB, LANES), BF16),
            pltpu.VMEM((SLAB, D), F32),
            pltpu.VMEM((4, HALF, D), F32),
            pltpu.VMEM((4, HALF, D), BF16),
            pltpu.VMEM((4, HALF, D), BF16),
            pltpu.VMEM((4, HALF, D), BF16),
            pltpu.VMEM((4, HALF, D), BF16),
            pltpu.VMEM((4, ROWS, D), BF16),
            pltpu.VMEM((4, ROWS, D), BF16),
            pltpu.VMEM((D, LANES), F32),
            pltpu.VMEM((4, 2, 2, PIECE, 128), BF16),
            pltpu.VMEM((4, 2, 2, PIECE, 128), BF16),
            pltpu.VMEM((2, 2, PIECE, 128), BF16),
            pltpu.VMEM((3, PIECE, 128), BF16),
            pltpu.VMEM((2, PIECE, 128), BF16),
            pltpu.VMEM((2, PIECE, 128), F32),
            pltpu.VMEM((PIECE, 128), F32),
            pltpu.VMEM((5, 4, 8, 128), F32),
            sem((15,)), sem((4, 4)),
            sem((4,)), sem((4,)),
            sem((17,)), sem((4, 2, 2)),
            sem, sem,
            sem((4,)), sem((4,)),
            sem((3,)), sem((4,)),
            sem((3,)), sem((4,)),
            sem((2, 3)), sem((4, 2)),
            sem((2, 2)), sem((2, 2)), sem((2,)),
            sem((5, 3)), sem((5, 4)),
        ],
        compiler_params=pltpu.CompilerParams(
            collective_id=0, has_side_effects=True, vmem_limit_bytes=48 * 1024 * 1024
        ),
        name="siglip",
    )(images, texts.T, logit_scale, bias)
    return loss[0, 0:1], grad_images, grad_texts.T


def solution(mesh):
    return jax.shard_map(
        per_device,
        mesh=mesh,
        in_specs=(P(("img", "txt"), None), P("txt", "img"), P(), P()),
        out_specs=(P(), P(("img", "txt"), None), P("txt", "img")),
        check_vma=False,
    )
```

```python
import jax
import jax.numpy as jnp
from jax import lax
from jax.experimental import pallas as pl
from jax.experimental.pallas import tpu as pltpu
from jax.sharding import PartitionSpec as P

EPS = 1e-06
F32 = jnp.float32
BF16 = jnp.bfloat16
MESH = pl.DeviceIdType.MESH
D = 1152
PAIRS = 9216
ROWS = 18
XPIECE = 168
HALF = 72
SLAB = 144
COLS = 72
TXT = 288
LANES = 384
DENSE = 168
PIECE = 176


def dot(a, b, dims):
    return lax.dot_general(a, b, (dims, ((), ())), preferred_element_type=F32)


def pack(data, inner):
    row = lax.broadcasted_iota(jnp.int32, (8, 128), 0)
    high = inner.astype(BF16).astype(F32)
    low = pltpu.roll(inner - high, 3, 0)
    tail = jnp.where(row < 3, high, jnp.where(row < 6, low, 0.0))
    return jnp.concatenate([data, tail], axis=0).astype(BF16)


def unpack(piece):
    wide = piece.astype(F32)
    tail = wide[DENSE:PIECE]
    return wide[:DENSE], tail + pltpu.roll(tail, 5, 0)


def densify(tiles):
    last = tiles[2]
    rest = last[0:24] + pltpu.roll(last[24:48], 32, 1) + pltpu.roll(last[48:72], 64, 1)
    return jnp.concatenate([tiles[0], tiles[1], rest], axis=0)


def last_tile(rest):
    lane = lax.broadcasted_iota(jnp.int32, (24, 128), 1)
    parts = [rest, pltpu.roll(rest, 96, 1), pltpu.roll(rest, 64, 1)]
    return jnp.concatenate([jnp.where(lane < 32, part, 0.0) for part in parts], axis=0)


def kernel(
    images, texts, scale, bias, loss_out, img_out, txt_out,
    xz, xg, xf, xs, tp, tpad, ts, tt, inv_own, inv_far, w1, w2, term, iown, ic_send, ic_recv, iy_send, iy_recv, iz_send, iz_recv,
    dtf, tx_send, tx_recv, tf_send, tf_recv, tg_recv, tsum, fin, ls,
    xz_ss, xz_rs, xc_ss, xc_rs, ts_ss, ts_rs, inv_ss, inv_rs, ic_ss, ic_rs, iy_ss, iy_rs, iz_ss, iz_rs,
    tx_ss, tx_rs, tf_ss, tf_rs, tg_rs, ls_ss, ls_rs,
):
    i = lax.axis_index("img")
    t = lax.axis_index("txt")
    x, zh, c = i // 4, (i // 2) % 2, i % 2
    y, zb, zm = t // 8, (t // 4) % 2, t % 4
    zbp, zhp, cp = 1 - zb, 1 - zh, 1 - c
    is_home = c == zb
    is_guest = c != zb

    def dev(x=x, zh=zh, c=c, y=y, zm=zm, zb=zb):
        return (x * 4 + zh * 2 + c, y * 8 + zb * 4 + zm)

    def turn(v, d):
        return lax.rem(v + d, 4)

    order = (1, 3, 2)
    peers = [dev(c=cp)]
    for cc in range(2):
        peers += [dev(zh=zhp, c=cc), dev(zb=zbp, c=cc), dev(zh=zhp, zb=zbp, c=cc)]
    for d in order:
        peers += [dev(x=turn(x, d)), dev(y=turn(y, d)), dev(zm=turn(zm, d))]
    barrier = pltpu.get_barrier_semaphore()
    for peer in peers:
        pl.semaphore_signal(barrier, inc=1, device_id=peer, device_id_type=MESH)

    pending = {"all": [], "home": [], "guest": []}

    def copy(src, dst, ss, rs, peer):
        return pltpu.make_async_remote_copy(
            src_ref=src, dst_ref=dst, send_sem=ss, recv_sem=rs, device_id=peer, device_id_type=MESH
        )

    def send(src, dst, ss, rs, peer, who="all", like=None):
        copy(src, dst, ss[0].at[ss[1:]] if ss[1:] else ss[0], rs, peer).start()
        pending[who].append((like or (lambda: src), ss))

    def sent(who):
        for like, ss in pending[who]:
            ref = like()
            copy(ref, ref, ss[0].at[ss[1:]] if ss[1:] else ss[0], ls_rs.at[0, 0], dev(c=cp)).wait_send()

    def arrived(ref, rs):
        copy(ref, ref, ls_ss.at[0, 0], rs, dev(c=cp)).wait_recv()

    sharpness = scale[0]
    offset = bias[0]

    def to_dense(block, first):
        for j in range(9):
            block[j * ROWS : (j + 1) * ROWS, :] = xf[first : first + ROWS, j * 128 : (j + 1) * 128]

    def from_dense(block, first):
        for j in range(9):
            xf[first : first + ROWS, j * 128 : (j + 1) * 128] = block[j * ROWS : (j + 1) * ROWS, :]

    xg[...] = jnp.zeros((8, XPIECE, 128), F32)
    own_image = images[...].astype(F32)
    img_norm = lax.rsqrt(jnp.sum(own_image * own_image, axis=1, keepdims=True) + EPS)
    xf[0:ROWS, :] = own_image * img_norm
    to_dense(xg.at[0], 0)
    xz[y, c, zm] = xg[0].astype(BF16)
    tpad[...] = jnp.zeros((COLS, LANES), F32)
    tpad[:, 0:TXT] = texts[...].astype(F32)
    tp[...] = densify([tpad[:, j * 128 : (j + 1) * 128] for j in range(3)]).astype(BF16)

    pl.semaphore_wait(barrier, len(peers))

    counts = {"home": 0, "guest": 0}

    def t_send(who, xx, h, cc, peer, own=False):
        k = counts[who]
        counts[who] += 1
        slot = ts.at[xx, h, cc]
        send(tp if own else slot, slot, (ts_ss, k), ts_rs.at[xx, h, cc], peer, who, lambda: tp)

    def t_wait(xx, h, cc):
        arrived(ts.at[xx, h, cc], ts_rs.at[xx, h, cc])

    def t_over_x(who, h, cc, own=False):
        for d in (2, 1, 3):
            t_send(who, x, h, cc, dev(x=turn(x, d)), own)

    x_count = [0]

    def x_send(q, peer):
        k = x_count[0]
        x_count[0] += 1
        slot = xz.at[y, c, q]
        send(slot, slot, (xz_ss, k), xz_rs.at[y, q], peer)

    def x_wait(yy, q):
        arrived(xz.at[yy, c, q], xz_rs.at[yy, q])

    def x_over_y(q):
        for d in (2, 1, 3):
            x_send(q, dev(y=turn(y, d)))

    def x_to_core(k, yy):
        group = xz.at[yy, c]
        send(group, group, (xc_ss, k), xc_rs.at[yy], dev(c=cp))

    @pl.when(is_home)
    def _():
        t_send("home", x, zh, c, dev(zb=zbp), True)
        t_send("home", x, zh, c, dev(zh=zhp, zb=zbp), True)
        t_over_x("home", zh, c, True)
        ts[x, zh, c] = tp[...]

    @pl.when(is_guest)
    def _():
        t_send("guest", x, zh, c, dev(zb=zbp, c=cp), True)
        t_send("guest", x, zh, c, dev(zh=zhp, zb=zbp, c=cp), True)
        t_send("guest", x, zh, c, dev(c=cp), True)

    x_over_y(zm)
    for who in ("home", "guest"):
        pending[who] = pending[who][2:]
    for k in range(2):
        copy(tp, tp, ts_ss.at[k], ls_rs.at[0, 0], dev(c=cp)).wait_send()
    for d in (1, 3, 2):
        x_send(zm, dev(zm=turn(zm, d)))

    @pl.when(is_home)
    def _():
        t_wait(x, zh, cp)
        t_over_x("home", zh, cp)

    @pl.when(is_guest)
    def _():
        for h in (zh, zhp):
            t_wait(x, h, zh)
            t_send("guest", x, h, zh, dev(zh=1 - h, zb=zbp))
            t_over_x("guest", h, zh)

    for d in order:
        x_wait(y, turn(zm, d))
        x_over_y(turn(zm, d))
    x_to_core(0, y)

    @pl.when(is_guest)
    def _():
        for h in (zh, zhp):
            t_wait(x, h, zhp)
            t_over_x("guest", h, zhp)

    @pl.when(is_home)
    def _():
        for cc in range(2):
            t_wait(x, zhp, cc)
            t_over_x("home", zhp, cc)

    for d in order:
        yy = turn(y, d)
        for q in range(4):
            x_wait(yy, turn(zm, q))
        x_to_core(d, yy)
    for d in (0, 1, 3, 2):
        yy = turn(y, d)
        arrived(xz.at[yy, cp], xc_rs.at[yy])
        xg[...] = xz[yy].reshape(8, XPIECE, 128).astype(F32)
        for q in range(8):
            from_dense(xg.at[q], q * ROWS)
        xs[yy] = xf[...].astype(BF16)

    square = jnp.zeros((8, LANES), F32)
    for h in (zh, zhp):
        for d in (0, 1, 3, 2):
            xx = turn(x, d)
            halves = []
            for cc in range(2):
                if d:
                    t_wait(xx, h, cc)
                block = ts[xx, h, cc].astype(F32)
                halves.append(jnp.concatenate([block[0:72], block[72:144], last_tile(block[144:DENSE])], axis=1))
            both = jnp.concatenate(halves, axis=0)
            tt[pl.ds(pl.multiple_of((xx * 2 + h) * 144, 16), 144), :] = both.astype(BF16)
            square += jnp.sum((both * both).reshape(18, 8, LANES), axis=0)
    inv_txt = lax.rsqrt(jnp.sum(square, axis=0, keepdims=True) + EPS)
    inv_own[...] = jnp.broadcast_to(inv_txt, (8, LANES))

    @pl.when(is_home)
    def _():
        send(inv_own, inv_far, (inv_ss,), inv_rs, dev(c=cp), "home")

    row = lax.broadcasted_iota(jnp.int32, (SLAB, LANES), 0)
    col = lax.broadcasted_iota(jnp.int32, (SLAB, LANES), 1)
    side = (row >= HALF).astype(jnp.int32)
    ahead = row + 504 * side - col + (x * 4 + zh * 2) * 576 + zb * 72 - (y * 8 + c * 4 + zm) * TXT
    valid = col < TXT
    loss_row = jnp.zeros((1, LANES), F32)
    inner = jnp.zeros((1, LANES), F32)

    for d in (0, 1, 3, 2):
        yy = turn(y, d)
        slab = xs[yy]
        raw = dot(slab, tt[...], ((1,), (0,)))
        logits = raw * (sharpness * inv_txt) + offset
        diagonal = ahead == -144 * yy
        sign = jnp.where(diagonal, -1.0, 1.0)
        u = sign * logits
        e = jnp.exp(-jnp.abs(u))
        soft = jnp.maximum(u, 0.0) + jnp.log1p(e)
        loss_row += jnp.sum(jnp.where(valid, soft, 0.0), axis=0, keepdims=True)
        w = sign * (jnp.where(u >= 0, 1.0, e) / (1.0 + e)) * sharpness
        w = jnp.where(valid, w, 0.0)
        wb = w.astype(BF16)
        inner += jnp.sum(wb.astype(F32) * raw, axis=0, keepdims=True)
        w1[yy] = wb
        w2[yy] = (w * inv_txt).astype(BF16)

    def loss_send(stage, place, others, value):
        ls[stage, place] = jnp.full((8, 128), value, F32)
        for k, peer in enumerate(others):
            send(ls.at[stage, place], ls.at[stage, place], (ls_ss, stage, k), ls_rs.at[stage, place], peer)

    def loss_wait(stage, places, n):
        for q in places:
            arrived(ls.at[stage, q], ls_rs.at[stage, q])
        total = ls[stage, 0]
        for q in range(1, n):
            total += ls[stage, q]
        return total

    loss_send(0, c, [dev(c=cp)], jnp.sum(loss_row))

    weights = w1[...].reshape(4 * SLAB, LANES)
    for q in range(3):
        part = xs[:, :, q * 384 : (q + 1) * 384].reshape(4 * SLAB, 384)
        dtf[q * 384 : (q + 1) * 384, :] = dot(part, weights, ((0,), (0,)))

    inner_tile = jnp.concatenate([inner[:, j * 128 : (j + 1) * 128] for j in range(3)] + [jnp.zeros((5, 128), F32)], axis=0)

    def features(xx, h, cc):
        rows = pl.ds(pl.multiple_of((xx * 4 + h * 2 + cc) * COLS, 8), COLS)
        return densify([dtf[rows, j * 128 : (j + 1) * 128] for j in range(3)])

    def which(j, m):
        h = jnp.where(is_home, (zhp, zh)[j], m)
        cc = jnp.where(is_home, m, (1 - zh, zh)[j])
        return h, cc

    for j in range(2):
        for d in (2, 1, 3):
            xx = turn(x, d)
            for m in range(2):
                tx_send[xx, j, m] = pack(features(xx, *which(j, m)), inner_tile)
            send(tx_send.at[xx, j], tx_recv.at[x, j], (tx_ss, j, d - 1), tx_rs.at[x, j], dev(x=xx))

    def from_core(k, yy):
        arrived(ic_recv.at[yy], ic_rs.at[yy])
        total = iown[yy] + ic_recv[yy].astype(F32)
        if k < 3:
            iy_send[yy] = total.astype(BF16)
            send(iy_send.at[yy], iy_recv.at[y], (iy_ss, k), iy_rs.at[y], dev(y=yy))
        return total

    before = None
    for k, d in enumerate((2, 1, 3, 0)):
        yy = turn(y, d)
        term[...] = dot(w2[yy], tt[...], ((1,), (1,)))
        ic_send[yy] = term[pl.ds(pl.multiple_of(cp * HALF, 8), HALF), :].astype(BF16)
        send(ic_send.at[yy], ic_recv.at[yy], (ic_ss, k), ic_rs.at[yy], dev(c=cp))
        iown[yy] = term[pl.ds(pl.multiple_of(c * HALF, 8), HALF), :]
        if before is not None:
            from_core(*before)
        before = (k, yy)

    total = from_core(*before)
    loss_v = loss_wait(0, [cp], 2)
    loss_send(1, zh * 2 + zb, [dev(zh=zhp), dev(zb=zbp), dev(zh=zhp, zb=zbp)], loss_v)
    def to_owners(j):
        sums = [features(x, *which(j, m)) for m in range(2)]
        inn = inner_tile
        for d in order:
            xx = turn(x, d)
            arrived(tx_recv.at[xx, j], tx_rs.at[xx, j])
            for m in range(2):
                more, more_inn = unpack(tx_recv[xx, j, m])
                sums[m] += more
            inn += more_inn
        if j == 0:
            for m in range(2):
                tf_send[0, m] = pack(sums[m], inn)

            @pl.when(is_home)
            def _():
                for m in range(2):
                    send(tf_send.at[0, m], tg_recv.at[zh], (tf_ss, 0, m), tg_rs.at[zh], dev(zh=m, zb=zbp),
                         "home", lambda: tf_send.at[0, 0])

            @pl.when(is_guest)
            def _():
                for m in range(2):
                    send(tf_send.at[0, m], tf_recv.at[zh], (tf_ss, 0, m), tf_rs.at[zh, 0], dev(zh=m, zb=zbp, c=1 - zh),
                         "guest", lambda: tf_send.at[0, 0])
        else:
            for m in range(2):
                tsum[m, 0:DENSE] = sums[m]
                tsum[m, DENSE:PIECE] = inn

            @pl.when(is_home)
            def _():
                tf_send[1, 0] = pack(tsum[cp, 0:DENSE], tsum[cp, DENSE:PIECE])
                send(tf_send.at[1, 0], tf_recv.at[2], (tf_ss, 1, 0), tf_rs.at[0, 1], dev(c=cp),
                     "home", lambda: tf_send.at[0, 0])
                fin[...] = tsum[c]

            @pl.when(is_guest)
            def _():
                for m in range(2):
                    arrived(tg_recv.at[1 - m], tg_rs.at[1 - m])
                    more, more_inn = unpack(tg_recv[1 - m])
                    tf_send[1, m] = pack(tsum[m, 0:DENSE] + more, tsum[m, DENSE:PIECE] + more_inn)
                    send(tf_send.at[1, m], tf_recv.at[zh], (tf_ss, 1, m), tf_rs.at[zh, 0], dev(zh=m, zb=zbp, c=zh),
                         "guest", lambda: tf_send.at[0, 0])

    to_owners(0)
    for d in order:
        q = turn(y, d)
        arrived(iy_recv.at[q], iy_rs.at[q])
        total += iy_recv[q].astype(F32)
    xf[0:HALF, :] = total
    for q in range(4):
        to_dense(xg.at[q], q * ROWS)
        iz_send[q] = xg[q].astype(BF16)
    for k, d in enumerate((2, 1, 3)):
        q = turn(zm, d)
        send(iz_send.at[q], iz_recv.at[zm], (iz_ss, k), iz_rs.at[zm], dev(zm=q))
    loss_v = loss_wait(1, [zhp * 2 + zb, zh * 2 + zbp, zhp * 2 + zbp], 4)
    loss_send(2, y, [dev(y=turn(y, d)) for d in order], loss_v)

    to_owners(1)
    loss_v = loss_wait(2, [turn(y, d) for d in order], 4)
    loss_send(3, zm, [dev(zm=turn(zm, d)) for d in order], loss_v)

    total = iz_send[zm].astype(F32)
    for d in order:
        q = turn(zm, d)
        arrived(iz_recv.at[q], iz_rs.at[q])
        total += iz_recv[q].astype(F32)
    xg[0] = total
    from_dense(xg.at[0], 0)
    total = xf[0:ROWS, :]
    own_image = images[...].astype(F32)
    img_norm = lax.rsqrt(jnp.sum(own_image * own_image, axis=1, keepdims=True) + EPS)
    img_inner = jnp.sum(own_image * total, axis=1, keepdims=True)
    img_out[...] = img_norm * total - own_image * (img_norm * img_norm * img_norm * img_inner)
    loss_v = loss_wait(3, [turn(zm, d) for d in order], 4)
    loss_send(4, x, [dev(x=turn(x, d)) for d in order], loss_v)

    @pl.when(is_guest)
    def _():
        arrived(inv_far, inv_rs)
        inv_own[...] = inv_far[...]
        arrived(tf_recv.at[2], tf_rs.at[0, 1])
        data, inn = unpack(tf_recv[2])
        fin[0:DENSE] = data
        fin[DENSE:PIECE] = inn

    data = fin[0:DENSE]
    inn = fin[DENSE:PIECE]
    for g in (1 - c, c):
        arrived(tf_recv.at[g], tf_rs.at[g, 0])
        more, more_inn = unpack(tf_recv[g])
        data += more
        inn += more_inn
    columns = (data[0:72], data[72:144], last_tile(data[144:DENSE]))
    for j in range(3):
        norm = inv_own[0:1, j * 128 : (j + 1) * 128]
        tpad[:, j * 128 : (j + 1) * 128] = norm * columns[j] - tpad[:, j * 128 : (j + 1) * 128] * (
            norm * norm * norm * inn[j : j + 1]
        )
    txt_out[...] = tpad[:, 0:TXT]
    loss_v = loss_wait(4, [turn(x, d) for d in order], 4)
    loss_out[...] = loss_v / PAIRS

    sent("all")

    @pl.when(is_home)
    def _():
        sent("home")

    @pl.when(is_guest)
    def _():
        sent("guest")


def per_device(images, texts, logit_scale, bias):
    vmem = pl.BlockSpec(memory_space=pltpu.VMEM)
    smem = pl.BlockSpec(memory_space=pltpu.SMEM)
    sem = pltpu.SemaphoreType.DMA
    loss, grad_images, grad_texts = pl.pallas_call(
        kernel,
        out_shape=(
            jax.ShapeDtypeStruct((8, 128), F32),
            jax.ShapeDtypeStruct((ROWS, D), F32),
            jax.ShapeDtypeStruct((COLS, TXT), F32),
        ),
        in_specs=[vmem, vmem, smem, smem],
        out_specs=(vmem, vmem, vmem),
        scratch_shapes=[
            pltpu.VMEM((4, 2, 4, XPIECE, 128), BF16),
            pltpu.VMEM((8, XPIECE, 128), F32),
            pltpu.VMEM((SLAB, D), F32),
            pltpu.VMEM((4, SLAB, D), BF16),
            pltpu.VMEM((DENSE, 128), BF16),
            pltpu.VMEM((COLS, LANES), F32),
            pltpu.VMEM((4, 2, 2, DENSE, 128), BF16),
            pltpu.VMEM((D, LANES), BF16),
            pltpu.VMEM((8, LANES), F32),
            pltpu.VMEM((8, LANES), F32),
            pltpu.VMEM((4, SLAB, LANES), BF16),
            pltpu.VMEM((4, SLAB, LANES), BF16),
            pltpu.VMEM((SLAB, D), F32),
            pltpu.VMEM((4, HALF, D), F32),
            pltpu.VMEM((4, HALF, D), BF16),
            pltpu.VMEM((4, HALF, D), BF16),
            pltpu.VMEM((4, HALF, D), BF16),
            pltpu.VMEM((4, HALF, D), BF16),
            pltpu.VMEM((4, XPIECE, 128), BF16),
            pltpu.VMEM((4, XPIECE, 128), BF16),
            pltpu.VMEM((D, LANES), F32),
            pltpu.VMEM((4, 2, 2, PIECE, 128), BF16),
            pltpu.VMEM((4, 2, 2, PIECE, 128), BF16),
            pltpu.VMEM((2, 2, PIECE, 128), BF16),
            pltpu.VMEM((3, PIECE, 128), BF16),
            pltpu.VMEM((2, PIECE, 128), BF16),
            pltpu.VMEM((2, PIECE, 128), F32),
            pltpu.VMEM((PIECE, 128), F32),
            pltpu.VMEM((5, 4, 8, 128), F32),
            sem((15,)), sem((4, 4)),
            sem((4,)), sem((4,)),
            sem((17,)), sem((4, 2, 2)),
            sem, sem,
            sem((4,)), sem((4,)),
            sem((3,)), sem((4,)),
            sem((3,)), sem((4,)),
            sem((2, 3)), sem((4, 2)),
            sem((2, 2)), sem((2, 2)), sem((2,)),
            sem((5, 3)), sem((5, 4)),
        ],
        compiler_params=pltpu.CompilerParams(
            collective_id=0, has_side_effects=True, vmem_limit_bytes=48 * 1024 * 1024
        ),
        name="siglip",
    )(images, texts.T, logit_scale, bias)
    return loss[0, 0:1], grad_images, grad_texts.T


def solution(mesh):
    return jax.shard_map(
        per_device,
        mesh=mesh,
        in_specs=(P(("img", "txt"), None), P("txt", "img"), P(), P()),
        out_specs=(P(), P(("img", "txt"), None), P("txt", "img")),
        check_vma=False,
    )
```

```python
import jax
import jax.numpy as jnp
from jax import lax
from jax.experimental import pallas as pl
from jax.experimental.pallas import tpu as pltpu
from jax.sharding import PartitionSpec as P

EPS = 1e-06
F32 = jnp.float32
BF16 = jnp.bfloat16
MESH = pl.DeviceIdType.MESH
D = 1152
PAIRS = 9216
ROWS = 18
XPIECE = 168
HALF = 72
SLAB = 144
COLS = 72
TXT = 288
LANES = 384
DENSE = 168
PIECE = 176


def dot(a, b, dims):
    return lax.dot_general(a, b, (dims, ((), ())), preferred_element_type=F32)


def pack(data, inner):
    row = lax.broadcasted_iota(jnp.int32, (8, 128), 0)
    high = inner.astype(BF16).astype(F32)
    low = pltpu.roll(inner - high, 3, 0)
    tail = jnp.where(row < 3, high, jnp.where(row < 6, low, 0.0))
    return jnp.concatenate([data, tail], axis=0).astype(BF16)


def unpack(piece):
    wide = piece.astype(F32)
    tail = wide[DENSE:PIECE]
    return wide[:DENSE], tail + pltpu.roll(tail, 5, 0)


def densify(tiles):
    last = tiles[2]
    rest = last[0:24] + pltpu.roll(last[24:48], 32, 1) + pltpu.roll(last[48:72], 64, 1)
    return jnp.concatenate([tiles[0], tiles[1], rest], axis=0)


def last_tile(rest):
    lane = lax.broadcasted_iota(jnp.int32, (24, 128), 1)
    parts = [rest, pltpu.roll(rest, 96, 1), pltpu.roll(rest, 64, 1)]
    return jnp.concatenate([jnp.where(lane < 32, part, 0.0) for part in parts], axis=0)


def kernel(
    images, texts, scale, bias, loss_out, img_out, txt_out,
    xz, xg, xf, xs, tp, tpad, ts, tt, inv_own, inv_far, w1, w2, term, iown, ic_send, ic_recv, iy_send, iy_recv, iz_send, iz_recv,
    dtf, tx_send, tx_recv, tf_send, tf_recv, tg_recv, tsum, fin, ls,
    xz_ss, xz_rs, xc_ss, xc_rs, ts_ss, ts_rs, inv_ss, inv_rs, ic_ss, ic_rs, iy_ss, iy_rs, iz_ss, iz_rs,
    tx_ss, tx_rs, tf_ss, tf_rs, tg_rs, ls_ss, ls_rs,
):
    i = lax.axis_index("img")
    t = lax.axis_index("txt")
    x, zh, c = i // 4, (i // 2) % 2, i % 2
    y, zb, zm = t // 8, (t // 4) % 2, t % 4
    zbp, zhp, cp = 1 - zb, 1 - zh, 1 - c
    is_home = c == zb
    is_guest = c != zb

    def dev(x=x, zh=zh, c=c, y=y, zm=zm, zb=zb):
        return (x * 4 + zh * 2 + c, y * 8 + zb * 4 + zm)

    def turn(v, d):
        return lax.rem(v + d, 4)

    order = (1, 3, 2)
    peers = [dev(c=cp)]
    for cc in range(2):
        peers += [dev(zh=zhp, c=cc), dev(zb=zbp, c=cc), dev(zh=zhp, zb=zbp, c=cc)]
    for d in order:
        peers += [dev(x=turn(x, d)), dev(y=turn(y, d)), dev(zm=turn(zm, d))]
    barrier = pltpu.get_barrier_semaphore()
    for peer in peers:
        pl.semaphore_signal(barrier, inc=1, device_id=peer, device_id_type=MESH)

    pending = {"all": [], "home": [], "guest": []}

    def copy(src, dst, ss, rs, peer):
        return pltpu.make_async_remote_copy(
            src_ref=src, dst_ref=dst, send_sem=ss, recv_sem=rs, device_id=peer, device_id_type=MESH
        )

    def send(src, dst, ss, rs, peer, who="all", like=None):
        copy(src, dst, ss[0].at[ss[1:]] if ss[1:] else ss[0], rs, peer).start()
        pending[who].append((like or (lambda: src), ss))

    def sent(who):
        for like, ss in pending[who]:
            ref = like()
            copy(ref, ref, ss[0].at[ss[1:]] if ss[1:] else ss[0], ls_rs.at[0, 0], dev(c=cp)).wait_send()

    def arrived(ref, rs):
        copy(ref, ref, ls_ss.at[0, 0], rs, dev(c=cp)).wait_recv()

    sharpness = scale[0]
    offset = bias[0]

    def to_dense(block, first):
        for j in range(9):
            block[j * ROWS : (j + 1) * ROWS, :] = xf[first : first + ROWS, j * 128 : (j + 1) * 128]

    def from_dense(block, first):
        for j in range(9):
            xf[first : first + ROWS, j * 128 : (j + 1) * 128] = block[j * ROWS : (j + 1) * ROWS, :]

    xg[...] = jnp.zeros((8, XPIECE, 128), F32)
    own_image = images[...].astype(F32)
    img_norm = lax.rsqrt(jnp.sum(own_image * own_image, axis=1, keepdims=True) + EPS)
    xf[0:ROWS, :] = own_image * img_norm
    to_dense(xg.at[0], 0)
    xz[y, c, zm] = xg[0].astype(BF16)
    tpad[...] = jnp.zeros((COLS, LANES), F32)
    tpad[:, 0:TXT] = texts[...].astype(F32)
    tp[...] = densify([tpad[:, j * 128 : (j + 1) * 128] for j in range(3)]).astype(BF16)

    pl.semaphore_wait(barrier, len(peers))

    counts = {"home": 0, "guest": 0}

    def t_send(who, xx, h, cc, peer, own=False):
        k = counts[who]
        counts[who] += 1
        slot = ts.at[xx, h, cc]
        send(tp if own else slot, slot, (ts_ss, k), ts_rs.at[xx, h, cc], peer, who, lambda: tp)

    def t_wait(xx, h, cc):
        arrived(ts.at[xx, h, cc], ts_rs.at[xx, h, cc])

    def t_over_x(who, h, cc, own=False):
        for d in (2, 1, 3):
            t_send(who, x, h, cc, dev(x=turn(x, d)), own)

    x_count = [0]

    def x_send(q, peer):
        k = x_count[0]
        x_count[0] += 1
        slot = xz.at[y, c, q]
        send(slot, slot, (xz_ss, k), xz_rs.at[y, q], peer)

    def x_wait(yy, q):
        arrived(xz.at[yy, c, q], xz_rs.at[yy, q])

    def x_over_y(q):
        for d in (2, 1, 3):
            x_send(q, dev(y=turn(y, d)))

    def x_to_core(k, yy):
        group = xz.at[yy, c]
        send(group, group, (xc_ss, k), xc_rs.at[yy], dev(c=cp))

    @pl.when(is_home)
    def _():
        t_send("home", x, zh, c, dev(zb=zbp), True)
        t_send("home", x, zh, c, dev(zh=zhp, zb=zbp), True)
        t_over_x("home", zh, c, True)
        ts[x, zh, c] = tp[...]

    @pl.when(is_guest)
    def _():
        t_send("guest", x, zh, c, dev(zb=zbp, c=cp), True)
        t_send("guest", x, zh, c, dev(zh=zhp, zb=zbp, c=cp), True)
        t_send("guest", x, zh, c, dev(c=cp), True)

    x_over_y(zm)
    for who in ("home", "guest"):
        pending[who] = pending[who][2:]
    for k in range(2):
        copy(tp, tp, ts_ss.at[k], ls_rs.at[0, 0], dev(c=cp)).wait_send()
    for d in (1, 3, 2):
        x_send(zm, dev(zm=turn(zm, d)))

    @pl.when(is_home)
    def _():
        t_wait(x, zh, cp)
        t_over_x("home", zh, cp)

    @pl.when(is_guest)
    def _():
        for h in (zh, zhp):
            t_wait(x, h, zh)
            t_send("guest", x, h, zh, dev(zh=1 - h, zb=zbp))
            t_over_x("guest", h, zh)

    for d in order:
        x_wait(y, turn(zm, d))
        x_over_y(turn(zm, d))
    x_to_core(0, y)

    @pl.when(is_guest)
    def _():
        for h in (zh, zhp):
            t_wait(x, h, zhp)
            t_over_x("guest", h, zhp)

    @pl.when(is_home)
    def _():
        for cc in range(2):
            t_wait(x, zhp, cc)
            t_over_x("home", zhp, cc)

    for d in order:
        yy = turn(y, d)
        for q in range(4):
            x_wait(yy, turn(zm, q))
        x_to_core(d, yy)
    for d in (0, 1, 3, 2):
        yy = turn(y, d)
        arrived(xz.at[yy, cp], xc_rs.at[yy])
        xg[...] = xz[yy].reshape(8, XPIECE, 128).astype(F32)
        for q in range(8):
            from_dense(xg.at[q], q * ROWS)
        xs[yy] = xf[...].astype(BF16)

    square = jnp.zeros((8, LANES), F32)
    for h in (zh, zhp):
        for d in (0, 1, 3, 2):
            xx = turn(x, d)
            halves = []
            for cc in range(2):
                if d:
                    t_wait(xx, h, cc)
                block = ts[xx, h, cc].astype(F32)
                halves.append(jnp.concatenate([block[0:72], block[72:144], last_tile(block[144:DENSE])], axis=1))
            both = jnp.concatenate(halves, axis=0)
            tt[pl.ds(pl.multiple_of((xx * 2 + h) * 144, 16), 144), :] = both.astype(BF16)
            square += jnp.sum((both * both).reshape(18, 8, LANES), axis=0)
    inv_txt = lax.rsqrt(jnp.sum(square, axis=0, keepdims=True) + EPS)
    inv_own[...] = jnp.broadcast_to(inv_txt, (8, LANES))

    @pl.when(is_home)
    def _():
        send(inv_own, inv_far, (inv_ss,), inv_rs, dev(c=cp), "home")

    row = lax.broadcasted_iota(jnp.int32, (SLAB, LANES), 0)
    col = lax.broadcasted_iota(jnp.int32, (SLAB, LANES), 1)
    side = (row >= HALF).astype(jnp.int32)
    ahead = row + 504 * side - col + (x * 4 + zh * 2) * 576 + zb * 72 - (y * 8 + c * 4 + zm) * TXT
    valid = col < TXT
    loss_row = jnp.zeros((1, LANES), F32)
    inner = jnp.zeros((1, LANES), F32)

    for d in (0, 1, 3, 2):
        yy = turn(y, d)
        slab = xs[yy]
        raw = dot(slab, tt[...], ((1,), (0,)))
        logits = raw * (sharpness * inv_txt) + offset
        diagonal = ahead == -144 * yy
        sign = jnp.where(diagonal, -1.0, 1.0)
        u = sign * logits
        e = jnp.exp(-jnp.abs(u))
        soft = jnp.maximum(u, 0.0) + jnp.log1p(e)
        loss_row += jnp.sum(jnp.where(valid, soft, 0.0), axis=0, keepdims=True)
        w = sign * (jnp.where(u >= 0, 1.0, e) / (1.0 + e)) * sharpness
        w = jnp.where(valid, w, 0.0)
        wb = w.astype(BF16)
        inner += jnp.sum(wb.astype(F32) * raw, axis=0, keepdims=True)
        w1[yy] = wb
        w2[yy] = (w * inv_txt).astype(BF16)

    def loss_send(stage, place, others, value):
        ls[stage, place] = jnp.full((8, 128), value, F32)
        for k, peer in enumerate(others):
            send(ls.at[stage, place], ls.at[stage, place], (ls_ss, stage, k), ls_rs.at[stage, place], peer)

    def loss_wait(stage, places, n):
        for q in places:
            arrived(ls.at[stage, q], ls_rs.at[stage, q])
        total = ls[stage, 0]
        for q in range(1, n):
            total += ls[stage, q]
        return total

    loss_send(0, c, [dev(c=cp)], jnp.sum(loss_row))

    weights = w1[...].reshape(4 * SLAB, LANES)
    for q in range(3):
        part = xs[:, :, q * 384 : (q + 1) * 384].reshape(4 * SLAB, 384)
        dtf[q * 384 : (q + 1) * 384, :] = dot(part, weights, ((0,), (0,)))

    inner_tile = jnp.concatenate([inner[:, j * 128 : (j + 1) * 128] for j in range(3)] + [jnp.zeros((5, 128), F32)], axis=0)

    def features(xx, h, cc):
        rows = pl.ds(pl.multiple_of((xx * 4 + h * 2 + cc) * COLS, 8), COLS)
        return densify([dtf[rows, j * 128 : (j + 1) * 128] for j in range(3)])

    def which(j, m):
        h = jnp.where(is_home, (zhp, zh)[j], m)
        cc = jnp.where(is_home, m, (1 - zh, zh)[j])
        return h, cc

    for j in range(2):
        for d in (2, 1, 3):
            xx = turn(x, d)
            for m in range(2):
                tx_send[xx, j, m] = pack(features(xx, *which(j, m)), inner_tile)
            send(tx_send.at[xx, j], tx_recv.at[x, j], (tx_ss, j, d - 1), tx_rs.at[x, j], dev(x=xx))

    def from_core(k, yy):
        arrived(ic_recv.at[yy], ic_rs.at[yy])
        total = iown[yy] + ic_recv[yy].astype(F32)
        if k < 3:
            iy_send[yy] = total.astype(BF16)
            send(iy_send.at[yy], iy_recv.at[y], (iy_ss, k), iy_rs.at[y], dev(y=yy))
        return total

    before = None
    for k, d in enumerate((2, 1, 3, 0)):
        yy = turn(y, d)
        term[...] = dot(w2[yy], tt[...], ((1,), (1,)))
        ic_send[yy] = term[pl.ds(pl.multiple_of(cp * HALF, 8), HALF), :].astype(BF16)
        send(ic_send.at[yy], ic_recv.at[yy], (ic_ss, k), ic_rs.at[yy], dev(c=cp))
        iown[yy] = term[pl.ds(pl.multiple_of(c * HALF, 8), HALF), :]
        if before is not None:
            from_core(*before)
        before = (k, yy)

    total = from_core(*before)
    loss_v = loss_wait(0, [cp], 2)
    loss_send(1, zh * 2 + zb, [dev(zh=zhp), dev(zb=zbp), dev(zh=zhp, zb=zbp)], loss_v)
    def to_owners(j):
        sums = [features(x, *which(j, m)) for m in range(2)]
        inn = inner_tile
        for d in order:
            xx = turn(x, d)
            arrived(tx_recv.at[xx, j], tx_rs.at[xx, j])
            for m in range(2):
                more, more_inn = unpack(tx_recv[xx, j, m])
                sums[m] += more
            inn += more_inn
        if j == 0:
            for m in range(2):
                tf_send[0, m] = pack(sums[m], inn)

            @pl.when(is_home)
            def _():
                for m in range(2):
                    send(tf_send.at[0, m], tg_recv.at[zh], (tf_ss, 0, m), tg_rs.at[zh], dev(zh=m, zb=zbp),
                         "home", lambda: tf_send.at[0, 0])

            @pl.when(is_guest)
            def _():
                for m in range(2):
                    send(tf_send.at[0, m], tf_recv.at[zh], (tf_ss, 0, m), tf_rs.at[zh, 0], dev(zh=m, zb=zbp, c=1 - zh),
                         "guest", lambda: tf_send.at[0, 0])
        else:
            for m in range(2):
                tsum[m, 0:DENSE] = sums[m]
                tsum[m, DENSE:PIECE] = inn

            @pl.when(is_home)
            def _():
                tf_send[1, 0] = pack(tsum[cp, 0:DENSE], tsum[cp, DENSE:PIECE])
                send(tf_send.at[1, 0], tf_recv.at[2], (tf_ss, 1, 0), tf_rs.at[0, 1], dev(c=cp),
                     "home", lambda: tf_send.at[0, 0])
                fin[...] = tsum[c]

            @pl.when(is_guest)
            def _():
                for m in range(2):
                    arrived(tg_recv.at[1 - m], tg_rs.at[1 - m])
                    more, more_inn = unpack(tg_recv[1 - m])
                    tf_send[1, m] = pack(tsum[m, 0:DENSE] + more, tsum[m, DENSE:PIECE] + more_inn)
                    send(tf_send.at[1, m], tf_recv.at[zh], (tf_ss, 1, m), tf_rs.at[zh, 0], dev(zh=m, zb=zbp, c=zh),
                         "guest", lambda: tf_send.at[0, 0])

    to_owners(0)
    loss_v = loss_wait(1, [zhp * 2 + zb, zh * 2 + zbp, zhp * 2 + zbp], 4)
    loss_send(2, y, [dev(y=turn(y, d)) for d in order], loss_v)
    for d in order:
        q = turn(y, d)
        arrived(iy_recv.at[q], iy_rs.at[q])
        total += iy_recv[q].astype(F32)
    xf[0:HALF, :] = total
    for q in range(4):
        to_dense(xg.at[q], q * ROWS)
        iz_send[q] = xg[q].astype(BF16)
    for k, d in enumerate((2, 1, 3)):
        q = turn(zm, d)
        send(iz_send.at[q], iz_recv.at[zm], (iz_ss, k), iz_rs.at[zm], dev(zm=q))
    loss_v = loss_wait(2, [turn(y, d) for d in order], 4)
    loss_send(3, zm, [dev(zm=turn(zm, d)) for d in order], loss_v)

    to_owners(1)
    loss_v = loss_wait(3, [turn(zm, d) for d in order], 4)
    loss_send(4, x, [dev(x=turn(x, d)) for d in order], loss_v)

    total = iz_send[zm].astype(F32)
    for d in order:
        q = turn(zm, d)
        arrived(iz_recv.at[q], iz_rs.at[q])
        total += iz_recv[q].astype(F32)
    xg[0] = total
    from_dense(xg.at[0], 0)
    total = xf[0:ROWS, :]
    own_image = images[...].astype(F32)
    img_norm = lax.rsqrt(jnp.sum(own_image * own_image, axis=1, keepdims=True) + EPS)
    img_inner = jnp.sum(own_image * total, axis=1, keepdims=True)
    img_out[...] = img_norm * total - own_image * (img_norm * img_norm * img_norm * img_inner)

    @pl.when(is_guest)
    def _():
        arrived(inv_far, inv_rs)
        inv_own[...] = inv_far[...]
        arrived(tf_recv.at[2], tf_rs.at[0, 1])
        data, inn = unpack(tf_recv[2])
        fin[0:DENSE] = data
        fin[DENSE:PIECE] = inn

    data = fin[0:DENSE]
    inn = fin[DENSE:PIECE]
    for g in (1 - c, c):
        arrived(tf_recv.at[g], tf_rs.at[g, 0])
        more, more_inn = unpack(tf_recv[g])
        data += more
        inn += more_inn
    columns = (data[0:72], data[72:144], last_tile(data[144:DENSE]))
    for j in range(3):
        norm = inv_own[0:1, j * 128 : (j + 1) * 128]
        tpad[:, j * 128 : (j + 1) * 128] = norm * columns[j] - tpad[:, j * 128 : (j + 1) * 128] * (
            norm * norm * norm * inn[j : j + 1]
        )
    txt_out[...] = tpad[:, 0:TXT]
    loss_v = loss_wait(4, [turn(x, d) for d in order], 4)
    loss_out[...] = loss_v / PAIRS

    sent("all")

    @pl.when(is_home)
    def _():
        sent("home")

    @pl.when(is_guest)
    def _():
        sent("guest")


def per_device(images, texts, logit_scale, bias):
    vmem = pl.BlockSpec(memory_space=pltpu.VMEM)
    smem = pl.BlockSpec(memory_space=pltpu.SMEM)
    sem = pltpu.SemaphoreType.DMA
    loss, grad_images, grad_texts = pl.pallas_call(
        kernel,
        out_shape=(
            jax.ShapeDtypeStruct((8, 128), F32),
            jax.ShapeDtypeStruct((ROWS, D), F32),
            jax.ShapeDtypeStruct((COLS, TXT), F32),
        ),
        in_specs=[vmem, vmem, smem, smem],
        out_specs=(vmem, vmem, vmem),
        scratch_shapes=[
            pltpu.VMEM((4, 2, 4, XPIECE, 128), BF16),
            pltpu.VMEM((8, XPIECE, 128), F32),
            pltpu.VMEM((SLAB, D), F32),
            pltpu.VMEM((4, SLAB, D), BF16),
            pltpu.VMEM((DENSE, 128), BF16),
            pltpu.VMEM((COLS, LANES), F32),
            pltpu.VMEM((4, 2, 2, DENSE, 128), BF16),
            pltpu.VMEM((D, LANES), BF16),
            pltpu.VMEM((8, LANES), F32),
            pltpu.VMEM((8, LANES), F32),
            pltpu.VMEM((4, SLAB, LANES), BF16),
            pltpu.VMEM((4, SLAB, LANES), BF16),
            pltpu.VMEM((SLAB, D), F32),
            pltpu.VMEM((4, HALF, D), F32),
            pltpu.VMEM((4, HALF, D), BF16),
            pltpu.VMEM((4, HALF, D), BF16),
            pltpu.VMEM((4, HALF, D), BF16),
            pltpu.VMEM((4, HALF, D), BF16),
            pltpu.VMEM((4, XPIECE, 128), BF16),
            pltpu.VMEM((4, XPIECE, 128), BF16),
            pltpu.VMEM((D, LANES), F32),
            pltpu.VMEM((4, 2, 2, PIECE, 128), BF16),
            pltpu.VMEM((4, 2, 2, PIECE, 128), BF16),
            pltpu.VMEM((2, 2, PIECE, 128), BF16),
            pltpu.VMEM((3, PIECE, 128), BF16),
            pltpu.VMEM((2, PIECE, 128), BF16),
            pltpu.VMEM((2, PIECE, 128), F32),
            pltpu.VMEM((PIECE, 128), F32),
            pltpu.VMEM((5, 4, 8, 128), F32),
            sem((15,)), sem((4, 4)),
            sem((4,)), sem((4,)),
            sem((17,)), sem((4, 2, 2)),
            sem, sem,
            sem((4,)), sem((4,)),
            sem((3,)), sem((4,)),
            sem((3,)), sem((4,)),
            sem((2, 3)), sem((4, 2)),
            sem((2, 2)), sem((2, 2)), sem((2,)),
            sem((5, 3)), sem((5, 4)),
        ],
        compiler_params=pltpu.CompilerParams(
            collective_id=0, has_side_effects=True, vmem_limit_bytes=48 * 1024 * 1024
        ),
        name="siglip",
    )(images, texts.T, logit_scale, bias)
    return loss[0, 0:1], grad_images, grad_texts.T


def solution(mesh):
    return jax.shard_map(
        per_device,
        mesh=mesh,
        in_specs=(P(("img", "txt"), None), P("txt", "img"), P(), P()),
        out_specs=(P(), P(("img", "txt"), None), P("txt", "img")),
        check_vma=False,
    )
```
